512 devices in a mesh: row: 32 (over z, core), col: 16 (over x, y).
Axes of the slice: x: 4, y: 4, z: 16, core: 2. Of those that a mesh axis runs over, the one named last changes fastest.
Arguments:
- factor: bfloat16 [2, 32, 4, 16, 256, 256], P(None, 'row', None, 'col'), may hold values from -0.0625 to 0.0625
- pattern: int32 [2, 32, 4, 16], P(None, 'row', None, 'col'), may hold values from 0 to 1
- dinv: bfloat16 [2, 32, 256, 256], P(None, 'row'), may hold values from -3 to 3
- rhs: float32 [2, 32, 256, 256], P(None, 'row'), may hold values from -6 to 6
Outputs:
- forward: bfloat16 [2, 32, 256, 256], P(None, 'row')
- solution: bfloat16 [2, 32, 256, 256], P(None, 'row')
The draws below stay inside these ranges and needn't reach their ends.
All inputs are finite; a program needn't handle non-finite values.
Results may differ from the reference program's by a relative error of at most 0.0075.
Values may be sent and summed in bfloat16 or wider, within the bound.
A program may use at most 64 MiB of HBM per device.

```python
import jax
import jax.numpy as jnp
from jax import lax

B = 256
R = 256
KR = 2
PROW = 32
PCOL = 16
K = 64
LEVELS = 4


def draw_pattern(key, part):
    count = KR * PROW
    key_rows = jax.random.fold_in(key, 11)
    key_cells = jax.random.fold_in(key, 12)
    density = jax.random.randint(key_rows, (count, 1), 1, 9)
    cells = jax.random.randint(key_cells, (count, count), 0, 8)
    present = (cells < density).astype(jnp.int32)
    return present.reshape(KR, PROW, LEVELS, PCOL)


def draw_dinv(key, part):
    key_diag = jax.random.fold_in(key, 21)
    key_off = jax.random.fold_in(key, 22)
    shape = (KR, PROW, B, B)
    diag = jnp.exp(jax.random.uniform(key_diag, (KR, PROW, B, 1), jnp.float32, -0.69, 0.69))
    off = jnp.clip(jax.random.normal(key_off, shape, jnp.float32), -4.0, 4.0) * (0.6 / B ** 0.5)
    rows = jnp.arange(B)[:, None]
    cols = jnp.arange(B)[None, :]
    strict = (rows > cols).astype(jnp.float32)
    eye = (rows == cols).astype(jnp.float32)
    return (off * strict + eye * diag).astype(jnp.bfloat16)


def block_levels(own_key, shape, shards, smallest, high):
    level, own = 1.0, jax.random.fold_in(own_key, 6)
    for axis_at, parts in shards:
        steps = jnp.exp(jax.random.uniform(jax.random.fold_in(own, axis_at), (parts,), jnp.float32, smallest / len(shards), high / len(shards)))
        level = level * jnp.repeat(steps, shape[axis_at] // parts).reshape([-1 if axis == axis_at else 1 for axis in range(len(shape))])
    return level


def gaussian(own_key, shape, width, most, pieces=(), held_as=jnp.bfloat16):
    gain = block_levels(own_key, shape, pieces, -0.22, 0.18) if pieces else 1.0
    drawn = jax.random.normal(own_key, shape, jnp.float32) * width * gain
    return jnp.minimum(jnp.maximum(drawn, -most), most).astype(held_as)


def setup_inputs(seed: int = 0) -> dict:
    seeds = jax.random.split(jax.random.key(seed), 5)
    return {
        "factor": gaussian(seeds[0], (KR, PROW, LEVELS, PCOL, B, B), (B * K // 2) ** -0.5, 0.0625, ((1, 32), (3, 16))),
        "pattern": draw_pattern(jax.random.fold_in(seeds[4], 71), 0),
        "dinv": draw_dinv(jax.random.fold_in(seeds[4], 71), 0),
        "rhs": gaussian(seeds[3], (KR, PROW, B, R), 1.0, 6.0, ((1, 32),), jnp.float32),
    }


def reference(factor, pattern, dinv, rhs):
    count = KR * PROW
    blocks = factor.reshape(count, count, B, B)
    level = jnp.arange(count, dtype=jnp.int32) // PCOL
    used = pattern.reshape(count, count) * (level[:, None] > level[None, :]).astype(jnp.int32)
    weights = used.astype(jnp.float32)
    inverse_blocks = dinv.reshape(count, B, B).astype(jnp.float32)
    right_side = rhs.reshape(count, B, R)
    upper_limit = lax.Precision.HIGHEST
    forward_solution = jnp.zeros((count, B, R), jnp.float32)
    for m in range(LEVELS):
        lower_bound = m * PCOL
        upper_bound = lower_bound + PCOL
        scaled_rows = blocks[lower_bound:upper_bound].astype(jnp.float32) * weights[lower_bound:upper_bound][:, :, None, None]
        partial_result = jnp.einsum('stkq,tqw->skw', scaled_rows, forward_solution, precision=upper_limit)
        level_target = jnp.einsum('pht,pty->phy', inverse_blocks[lower_bound:upper_bound], right_side[lower_bound:upper_bound] - partial_result, precision=upper_limit)
        forward_solution = forward_solution.at[lower_bound:upper_bound].set(level_target.astype(jnp.bfloat16).astype(jnp.float32))
    backward_solution = jnp.zeros((count, B, R), jnp.float32)
    for m in range(LEVELS - 1, -1, -1):
        lower_bound = m * PCOL
        upper_bound = lower_bound + PCOL
        scaled_rows = blocks[:, lower_bound:upper_bound].astype(jnp.float32) * weights[:, lower_bound:upper_bound][:, :, None, None]
        partial_result = jnp.einsum('tlcn,tce->lne', scaled_rows, backward_solution, precision=upper_limit)
        level_unknowns = jnp.einsum('wst,wsx->wtx', inverse_blocks[lower_bound:upper_bound], forward_solution[lower_bound:upper_bound] - partial_result, precision=upper_limit)
        backward_solution = backward_solution.at[lower_bound:upper_bound].set(level_unknowns.astype(jnp.bfloat16).astype(jnp.float32))
    forward = forward_solution.astype(jnp.bfloat16).reshape(KR, PROW, B, R)
    solution = backward_solution.astype(jnp.bfloat16).reshape(KR, PROW, B, R)
    return (forward, solution)
```

```python
import jax
import jax.numpy as jnp
from jax import lax
from jax.experimental import pallas as pl
from jax.experimental.pallas import tpu as pltpu
from jax.sharding import PartitionSpec as P

MESH = pl.DeviceIdType.MESH
NT = (((1,), (1,)), ((), ()))
NN = (((1,), (0,)), ((), ()))
Y_IN, P_IN, Y_ALL, X_IN, X_OTH, Q_IN, L_IN = 0, 3, 5, 7, 9, 11, 14


def exact_dot(lhs, inverse, dims):
    rows = lhs.shape[0]
    high = lhs.astype(jnp.bfloat16)
    rest = lhs - high.astype(jnp.float32)
    mid = rest.astype(jnp.bfloat16)
    low = (rest - mid.astype(jnp.float32)).astype(jnp.bfloat16)
    stacked = jnp.concatenate([high, mid, low], axis=0)
    out = lax.dot_general(stacked, inverse, dims, preferred_element_type=jnp.float32)
    return out[:rows] + (out[rows : 2 * rows] + out[2 * rows :])


def kernel(
    pattern, factor, dinv, rhs, out_y, out_x,
    blocks, b_t, y_own, x_own, y_in, p_out, p_in, acc, y_all, x_in, x_oth, q_acc, q_out, q_in,
    send_sem, recv_sem,
):
    r, c = lax.axis_index("row"), lax.axis_index("col")
    z, k = r // 2, r % 2
    h = z // 8
    s = r % 16
    kq, ql = c // 8, c % 8
    barrier = pltpu.get_barrier_semaphore()

    def signal(row, col):
        here = (row == r) & (col == c)

        @pl.when(jnp.logical_not(here))
        def _():
            pl.semaphore_signal(barrier, inc=1, device_id=(row, col), device_id_type=MESH)

    @pl.loop(0, 16)
    def _(p):
        signal(2 * ((z + p) % 16) + kq, s)
        signal(c + 16 * (p // 8), 8 * k + p % 8)

    @pl.loop(0, 16)
    def _(p):
        signal(r, (c + p) % 16)
        signal(2 * z + 1 - k, (c + p) % 16)

    def remote(src, dst, event, cls, row, col):
        return pltpu.make_async_remote_copy(
            src_ref=src, dst_ref=dst, send_sem=send_sem.at[event], recv_sem=recv_sem.at[cls],
            device_id=(row, col), device_id_type=MESH,
        )

    def send(src, dst, event, cls, row, col, here):
        @pl.when(here)
        def _():
            pltpu.make_async_copy(src, dst, recv_sem.at[cls]).start()

        @pl.when(jnp.logical_not(here))
        def _():
            remote(src, dst, event, cls, row, col).start()

    def arrived(buf, cls):
        remote(buf, buf, 0, cls, r, c).wait_recv()

    def sent(event, count, one_less):
        @pl.when(one_less)
        def _():
            if count > 1:
                d = y_all.at[0, pl.ds(0, count - 1)]
                remote(d, d, event, 0, r, c).wait_send()

        @pl.when(jnp.logical_not(one_less))
        def _():
            d = y_all.at[0, pl.ds(0, count)]
            remote(d, d, event, 0, r, c).wait_send()

    def to_column(src, level, half, event):
        def go(p, here):
            row = 2 * (8 * half + (z + p) % 8) + kq
            args = (src, y_in.at[level, ql], event, Y_IN + level, row, s)
            if here is None:
                remote(*args).start()
            else:
                send(*args, here)

        go(0, (half == h) & (kq == k) & (s == c))

        @pl.loop(1, 8)
        def _(p):
            go(p, None)

    def column_self(half):
        return (half == h) & (kq == k) & (s == c)

    def to_owner(slot, event):
        for kk in range(2):
            for p in range(1):
                send(p_out.at[slot, kk, ql], p_in.at[slot, c], event, P_IN + slot,
                     2 * z + kk, 8 * k + ql, (kk == k) & (kq == k))

        @pl.loop(1, 8)
        def _(p):
            part = (ql + p) % 8
            for kk in range(2):
                remote(p_out.at[slot, kk, part], p_in.at[slot, c], event, P_IN + slot,
                       2 * z + kk, 8 * k + part).start()

    def to_plane(src, dst, event, cls, core):
        send(src, dst, event, cls, 2 * z + core, c, core == k)

        @pl.loop(1, 16)
        def _(p):
            remote(src, dst, event, cls, 2 * z + core, (c + p) % 16).start()

    def to_supernode(slot, cls, half, event):
        row = 16 * half + c

        def go(part, here):
            args = (q_out.at[slot, part], q_in.at[cls, z % 8], event, Q_IN + cls, row, 8 * k + part)
            if here is None:
                remote(*args).start()
            else:
                send(*args, here)

        go(ql, supernode_self(half))

        @pl.loop(1, 8)
        def _(p):
            go((ql + p) % 8, None)

    def supernode_self(half):
        return (16 * half + c == r) & (kq == k)

    def product(level, kk, index):
        y = y_in[level].reshape(128, 256)
        return lax.dot_general(y, blocks[kk, index], NT, preferred_element_type=jnp.float32)

    def back_product(slot, index):
        total = None
        for kk in range(2):
            x = x_in[slot, kk].reshape(128, 256)
            term = lax.dot_general(x, blocks[kk, index], NN, preferred_element_type=jnp.float32)
            total = term if total is None else total + term
        return total

    def total_of(buf):
        return jnp.sum(buf[...].astype(jnp.float32), axis=0)

    def solve_forward(slot):
        arrived(p_in.at[slot], P_IN + slot)
        residue = b_t[slot] - total_of(p_in.at[slot])
        y_own[slot] = exact_dot(residue, dinv[slot], NT).astype(jnp.bfloat16)

    def put_q(slot, value):
        q_out[slot] = value.astype(jnp.bfloat16).reshape(8, 16, 256)

    def natural(value):
        return value.astype(jnp.float32).T.astype(jnp.bfloat16)

    def write_y(slot):
        arrived(y_all.at[slot], Y_ALL + slot)
        out_y[slot] = natural(y_all[slot].reshape(256, 256))

    def write_x(slot):
        arrived(x_oth.at[slot], X_OTH + slot)
        mine = x_in[slot, k].reshape(128, 256)
        other = x_oth[slot].reshape(128, 256)

        @pl.when(k == 0)
        def _():
            out_x[slot] = natural(jnp.concatenate([mine, other], axis=0))

        @pl.when(k == 1)
        def _():
            out_x[slot] = natural(jnp.concatenate([other, mine], axis=0))

    def spread_x(slot, event):
        to_plane(x_own.at[slot], x_in.at[slot, k, ql], event, X_IN + slot, kq)

        @pl.when(kq != k)
        def _():
            to_plane(x_own.at[slot], x_oth.at[slot, ql], event + 1, X_OTH + slot, k)

    def spread_x_sent(event):
        sent(event, 16, kq == k)

        @pl.when(kq != k)
        def _():
            sent(event + 1, 15, False)

    for slot in range(2):
        q_acc[...] = rhs[slot].T
        b_t[slot] = q_acc[pl.ds(pl.multiple_of(16 * c, 16), 16), :]

    @pl.when(h == 0)
    def _():
        y_own[0] = exact_dot(b_t[0], dinv[0], NT).astype(jnp.bfloat16)

    places = ((0, 0), (1, 0), (1, 1), (1, 2))
    for index, (slot, level) in enumerate(places):
        weight = pattern[slot, level].astype(jnp.float32)
        blocks[k, index] = (factor[slot, level].astype(jnp.float32) * weight).astype(jnp.bfloat16)

    pl.semaphore_wait(barrier, 63 - 2 * ((kq == k) & (s == c)).astype(jnp.int32))

    swap = remote(blocks.at[k], blocks.at[k], 0, L_IN, 2 * z + 1 - k, c)

    @pl.when(h == 0)
    def _():
        to_column(y_own.at[0], 0, 1, 1)
        swap.start()
        to_column(y_own.at[0], 0, 0, 2)
        out_y[0] = exact_dot(rhs[0].T, dinv[0], NT).T.astype(jnp.bfloat16)
        arrived(blocks.at[1 - k], L_IN)
        arrived(y_in.at[0], Y_IN)
        for kk in range(2):
            acc[kk] = product(0, kk, 1)
        arrived(y_in.at[1], Y_IN + 1)
        for kk in range(2):
            value = acc[kk] + product(1, kk, 2)
            p_out[1, kk] = value.astype(jnp.bfloat16).reshape(8, 16, 256)
        to_owner(1, 3)
        solve_forward(1)
        to_column(y_own.at[1], 2, 1, 4)
        to_plane(y_own.at[1], y_all.at[1, c], 5, Y_ALL + 1, k)
        write_y(1)
        arrived(q_in.at[2], Q_IN + 2)
        residue = y_own[1].astype(jnp.float32) - total_of(q_in.at[2])
        x_own[1] = exact_dot(residue, dinv[1], NN).astype(jnp.bfloat16)
        spread_x(1, 6)
        arrived(x_in.at[1], X_IN + 1)
        put_q(0, back_product(1, 2))
        to_supernode(0, 1, 1, 8)
        put_q(1, back_product(1, 1))
        to_supernode(1, 0, 0, 9)
        write_x(1)
        arrived(q_in.at[0], Q_IN)
        residue = y_own[0].astype(jnp.float32) - total_of(q_in.at[0])
        arrived(q_in.at[1], Q_IN + 1)
        residue = residue - total_of(q_in.at[1])
        x_own[0] = exact_dot(residue, dinv[0], NN).astype(jnp.bfloat16)

        @pl.when(kq == k)
        def _():
            to_plane(x_own.at[0], x_in.at[0, k, ql], 10, X_IN, k)

        @pl.when(kq != k)
        def _():
            to_plane(x_own.at[0], x_oth.at[0, ql], 10, X_OTH, k)

        arrived(x_in.at[0, k], X_IN)
        write_x(0)
        swap.wait_send()
        sent(1, 8, False)
        sent(2, 8, column_self(0))
        sent(3, 16, kq == k)
        sent(4, 8, False)
        sent(5, 15, False)
        spread_x_sent(6)
        sent(8, 8, False)
        sent(9, 8, supernode_self(0))
        sent(10, 15, False)

    @pl.when(h == 1)
    def _():
        swap.start()
        arrived(blocks.at[1 - k], L_IN)
        arrived(y_in.at[0], Y_IN)
        for kk in range(2):
            p_out[0, kk] = product(0, kk, 0).astype(jnp.bfloat16).reshape(8, 16, 256)
        to_owner(0, 1)
        solve_forward(0)
        to_column(y_own.at[0], 1, 0, 2)
        to_column(y_own.at[0], 1, 1, 3)
        to_plane(y_own.at[0], y_all.at[0, c], 4, Y_ALL, k)
        for kk in range(2):
            acc[kk] = product(0, kk, 1)
        arrived(y_in.at[1], Y_IN + 1)
        for kk in range(2):
            acc[kk] += product(1, kk, 2)
        write_y(0)
        arrived(y_in.at[2], Y_IN + 2)
        for kk in range(2):
            value = acc[kk] + product(2, kk, 3)
            p_out[1, kk] = value.astype(jnp.bfloat16).reshape(8, 16, 256)
        to_owner(1, 5)
        solve_forward(1)
        x_own[1] = exact_dot(y_own[1].astype(jnp.float32), dinv[1], NN).astype(jnp.bfloat16)
        spread_x(1, 6)
        to_plane(y_own.at[1], y_all.at[1, c], 8, Y_ALL + 1, k)
        arrived(x_in.at[1], X_IN + 1)
        put_q(0, back_product(1, 3))
        to_supernode(0, 2, 0, 9)
        put_q(1, back_product(1, 2))
        to_supernode(1, 0, 1, 10)
        acc[0] = back_product(1, 1)
        write_y(1)
        write_x(1)
        arrived(q_in.at[0], Q_IN)
        residue = y_own[0].astype(jnp.float32) - total_of(q_in.at[0])
        arrived(q_in.at[1], Q_IN + 1)
        residue = residue - total_of(q_in.at[1])
        x_own[0] = exact_dot(residue, dinv[0], NN).astype(jnp.bfloat16)
        spread_x(0, 11)
        arrived(x_in.at[0], X_IN)
        put_q(2, acc[0] + back_product(0, 0))
        to_supernode(2, 1, 0, 13)
        write_x(0)
        swap.wait_send()
        sent(1, 16, kq == k)
        sent(2, 8, False)
        sent(3, 8, column_self(1))
        sent(4, 15, False)
        sent(5, 16, kq == k)
        spread_x_sent(6)
        sent(8, 15, False)
        sent(9, 8, False)
        sent(10, 8, supernode_self(1))
        spread_x_sent(11)
        sent(13, 8, False)


def per_device(factor, pattern, dinv, rhs):
    bf16, f32 = jnp.bfloat16, jnp.float32
    vmem = pl.BlockSpec(memory_space=pltpu.VMEM)
    out = jax.ShapeDtypeStruct((2, 256, 256), bf16)
    forward, back = pl.pallas_call(
        kernel,
        out_shape=(out, out),
        in_specs=[pl.BlockSpec(memory_space=pltpu.SMEM), vmem, vmem, vmem],
        out_specs=(vmem, vmem),
        scratch_shapes=[
            pltpu.VMEM((2, 4, 256, 256), bf16),
            pltpu.VMEM((2, 16, 256), f32),
            pltpu.VMEM((2, 16, 256), bf16),
            pltpu.VMEM((2, 16, 256), bf16),
            pltpu.VMEM((3, 8, 16, 256), bf16),
            pltpu.VMEM((2, 2, 8, 16, 256), bf16),
            pltpu.VMEM((2, 16, 16, 256), bf16),
            pltpu.VMEM((2, 128, 256), f32),
            pltpu.VMEM((2, 16, 16, 256), bf16),
            pltpu.VMEM((2, 2, 8, 16, 256), bf16),
            pltpu.VMEM((2, 8, 16, 256), bf16),
            pltpu.VMEM((256, 256), f32),
            pltpu.VMEM((3, 8, 16, 256), bf16),
            pltpu.VMEM((3, 8, 16, 256), bf16),
            pltpu.SemaphoreType.DMA((14,)),
            pltpu.SemaphoreType.DMA((15,)),
        ],
        compiler_params=pltpu.CompilerParams(
            collective_id=0, has_side_effects=True, vmem_limit_bytes=32 * 1024 * 1024
        ),
        cost_estimate=pl.CostEstimate(flops=600_000_000, bytes_accessed=3_000_000, transcendentals=0),
    )(pattern[:, 0, :, 0], factor[:, 0, :, 0], dinv[:, 0], rhs[:, 0])
    return forward[:, None], back[:, None]


def solution(mesh):
    placed = (
        P(None, "row", None, "col", None, None),
        P(None, "row", None, "col"),
        P(None, "row", None, None),
        P(None, "row", None, None),
    )
    return jax.shard_map(
        per_device,
        mesh=mesh,
        in_specs=placed,
        out_specs=(P(None, "row", None, None), P(None, "row", None, None)),
        check_vma=False,
    )
```

```python
import jax
import jax.numpy as jnp
from jax import lax
from jax.experimental import pallas as pl
from jax.experimental.pallas import tpu as pltpu
from jax.sharding import PartitionSpec as P

MESH = pl.DeviceIdType.MESH
NT = (((1,), (1,)), ((), ()))
NN = (((1,), (0,)), ((), ()))
PLACES = ((0, 0), (1, 0), (1, 1), (1, 2))
Y_IN, P_IN, Y_ALL, X_IN, X_ALL, Q_IN, L_IN, G_IN = 0, 3, 5, 7, 9, 11, 14, 18


def exact_dot(lhs, inverse, dims):
    rows = lhs.shape[0]
    high = lhs.astype(jnp.bfloat16)
    rest = lhs - high.astype(jnp.float32)
    mid = rest.astype(jnp.bfloat16)
    low = (rest - mid.astype(jnp.float32)).astype(jnp.bfloat16)
    stacked = jnp.concatenate([high, mid, low], axis=0)
    out = lax.dot_general(stacked, inverse, dims, preferred_element_type=jnp.float32)
    return out[:rows] + (out[rows : 2 * rows] + out[2 * rows :])


def kernel(
    pattern_hbm, factor_hbm, dinv_hbm, rhs_hbm, out_y, out_x,
    pattern, factor, dinv, rhs, blocks, b_t, y_own, x_own, y_in, p_out, p_in, acc,
    y_all, x_in, x_all, turned, q_acc, q_out, q_in,
    send_sem, recv_sem, load_sem,
):
    r, c = lax.axis_index("row"), lax.axis_index("col")
    z, k = r // 2, r % 2
    h = z // 8
    s = r % 16
    x, y = c // 4, c % 4
    kq, ql = y // 2, y % 2
    barrier = pltpu.get_barrier_semaphore()
    loads = [
        pltpu.make_async_copy(source, target, load_sem.at[i])
        for i, (source, target) in enumerate(
            ((rhs_hbm, rhs), (dinv_hbm, dinv), (pattern_hbm, pattern))
            + tuple((factor_hbm.at[slot, level], factor.at[j]) for j, (slot, level) in enumerate(PLACES))
        )
    ]
    for load in loads:
        load.start()

    def signal(row, col):
        here = (row == r) & (col == c)

        @pl.when(jnp.logical_not(here))
        def _():
            pl.semaphore_signal(barrier, inc=1, device_id=(row, col), device_id_type=MESH)

    @pl.loop(0, 16)
    def _(p):
        signal(2 * ((z + p) % 16) + kq, 4 * x + s % 4)
        signal(16 * (p // 8) + 4 * (p // 2 % 4) + y, 4 * x + 2 * k + p % 2)

    @pl.loop(0, 16)
    def _(p):
        signal(r, (c + p) % 16)
        signal(2 * z + 1 - k, (c + p) % 16)

    def remote(src, dst, event, cls, row, col):
        return pltpu.make_async_remote_copy(
            src_ref=src, dst_ref=dst, send_sem=send_sem.at[event], recv_sem=recv_sem.at[cls],
            device_id=(row, col), device_id_type=MESH,
        )

    def send(src, dst, event, cls, row, col, here):
        @pl.when(here)
        def _():
            pltpu.make_async_copy(src, dst, recv_sem.at[cls]).start()

        @pl.when(jnp.logical_not(here))
        def _():
            remote(src, dst, event, cls, row, col).start()

    def arrived(buf, cls):
        remote(buf, buf, 0, cls, r, c).wait_recv()

    def sent(event, count, one_less):
        @pl.when(one_less)
        def _():
            if count > 1:
                d = y_all.at[0, pl.ds(0, count - 1)]
                remote(d, d, event, 0, r, c).wait_send()

        @pl.when(jnp.logical_not(one_less))
        def _():
            d = y_all.at[0, pl.ds(0, count)]
            remote(d, d, event, 0, r, c).wait_send()

    def to_column(src, level, half, event):
        def go(p, here):
            row = 2 * (8 * half + (z + p) % 8) + kq
            args = (src, y_in.at[level, s // 4, ql], event, Y_IN + level, row, 4 * x + s % 4)
            if here is None:
                remote(*args).start()
            else:
                send(*args, here)

        go(0, own_column(half))

        @pl.loop(1, 8)
        def _(p):
            go(p, None)

    def own_column(half):
        return (half == h) & (kq == k) & (s % 4 == y)

    def to_owner(slot, event):
        for p in range(2):
            part = (ql + p) % 2
            for kk in range(2):
                args = (p_out.at[slot, kk, part], p_in.at[slot, y], event, P_IN + slot,
                        2 * z + kk, 4 * x + 2 * k + part)
                if p == 0:
                    send(*args, (kk == k) & (kq == k))
                else:
                    remote(*args).start()

    def to_line(src, slot, event):
        for p in range(4):
            args = (src, x_in.at[slot, k, ql], event, X_IN + slot, 2 * z + kq, 4 * x + (y + p) % 4)
            if p == 0:
                send(*args, kq == k)
            else:
                remote(*args).start()

    def to_plane(src, dst, event, cls):
        pltpu.make_async_copy(src, dst, recv_sem.at[cls]).start()

        @pl.loop(1, 16)
        def _(p):
            remote(src, dst, event, cls, r, (c + p) % 16).start()

    def to_supernode(slot, cls, half, event):
        def go(p, here):
            line, part = (s // 4 + p // 2) % 4, (ql + p) % 2
            args = (q_out.at[slot, line, part], q_in.at[cls, z % 8], event, Q_IN + cls,
                    16 * half + 4 * line + y, 4 * x + 2 * k + part)
            if here is None:
                remote(*args).start()
            else:
                send(*args, here)

        go(0, own_column(half))

        @pl.loop(1, 8)
        def _(p):
            go(p, None)

    def gather(index):
        for p in range(1, 4):
            block = blocks.at[k, index, x]
            remote(block, block, 14 + index, G_IN + index, r, 4 * ((x + p) % 4) + y).start()

    def swap(index):
        return remote(blocks.at[k, index], blocks.at[k, index], 18 + index, L_IN + index, 2 * z + 1 - k, c)

    def gathered(index):
        arrived(blocks.at[k, index, pl.ds(0, 3)], G_IN + index)
        swap(index).start()

    def factor_ready(index):
        arrived(blocks.at[1 - k, index], L_IN + index)

    def factor_sent(index):
        d = blocks.at[k, index, pl.ds(0, 3)]
        remote(d, d, 14 + index, 0, r, c).wait_send()
        swap(index).wait_send()

    def product(level, kk, index):
        total = None
        for line in range(4):
            term = lax.dot_general(
                y_in[level, line].reshape(32, 256), blocks[kk, index, line], NT,
                preferred_element_type=jnp.float32,
            )
            total = term if total is None else total + term
        return total

    def back_product(slot, index, line):
        total = None
        for kk in range(2):
            term = lax.dot_general(
                x_in[slot, kk].reshape(32, 256), blocks[kk, index, line], NN,
                preferred_element_type=jnp.float32,
            )
            total = term if total is None else total + term
        return total

    def total_of(buf):
        return jnp.sum(buf[...].astype(jnp.float32), axis=0)

    def solve_forward(slot):
        arrived(p_in.at[slot], P_IN + slot)
        residue = b_t[slot] - total_of(p_in.at[slot])
        y_own[slot] = exact_dot(residue, dinv[slot], NT).astype(jnp.bfloat16)

    def put_p(slot, kk, value):
        p_out[slot, kk] = value.astype(jnp.bfloat16).reshape(2, 16, 256)

    def put_q(slot, line, value):
        q_out[slot, line] = value.astype(jnp.bfloat16).reshape(2, 16, 256)

    def natural(value):
        return value.reshape(256, 256).astype(jnp.float32).T.astype(jnp.bfloat16)

    def write_y(slot):
        arrived(y_all.at[slot], Y_ALL + slot)
        out_y[slot] = natural(y_all[slot])

    def write_x(slot):
        arrived(x_all.at[slot], X_ALL + slot)
        out_x[slot] = natural(x_all[slot])

    loads[0].wait()
    for slot in range(2):
        turned[...] = rhs[slot].T
        b_t[slot] = turned[pl.ds(pl.multiple_of(16 * c, 16), 16), :]

    loads[1].wait()

    @pl.when(h == 0)
    def _():
        y_own[0] = exact_dot(b_t[0], dinv[0], NT).astype(jnp.bfloat16)

    for load in loads[2:]:
        load.wait()
    for index, (slot, level) in enumerate(PLACES):
        weight = pattern[slot, level].astype(jnp.float32)
        blocks[k, index, x] = (factor[index].astype(jnp.float32) * weight).astype(jnp.bfloat16)

    pl.semaphore_wait(barrier, 63 - 2 * ((kq == k) & (s % 4 == y)).astype(jnp.int32))

    @pl.when(h == 0)
    def _():
        to_column(y_own.at[0], 0, 1, 1)
        gather(1)
        gather(2)
        sent(1, 8, False)
        to_column(y_own.at[0], 0, 0, 2)
        out_y[0] = exact_dot(rhs[0].T, dinv[0], NT).T.astype(jnp.bfloat16)
        gathered(1)
        gathered(2)
        factor_ready(1)
        arrived(y_in.at[0], Y_IN)
        for kk in range(2):
            acc[kk] = product(0, kk, 1)
        factor_ready(2)
        arrived(y_in.at[1], Y_IN + 1)
        for kk in range(2):
            put_p(1, kk, acc[kk] + product(1, kk, 2))
        to_owner(1, 3)
        solve_forward(1)
        to_column(y_own.at[1], 2, 1, 4)
        sent(4, 8, False)
        to_plane(y_own.at[1], y_all.at[1, c], 5, Y_ALL + 1)
        write_y(1)
        arrived(q_in.at[2], Q_IN + 2)
        residue = y_own[1].astype(jnp.float32) - total_of(q_in.at[2])
        x_own[1] = exact_dot(residue, dinv[1], NN).astype(jnp.bfloat16)
        to_line(x_own.at[1], 1, 6)
        arrived(x_in.at[1], X_IN + 1)
        for line in range(4):
            put_q(0, line, back_product(1, 2, line))
        to_supernode(0, 1, 1, 8)
        for line in range(4):
            put_q(1, line, back_product(1, 1, line))
        to_supernode(1, 0, 0, 9)
        to_plane(x_own.at[1], x_all.at[1, c], 7, X_ALL + 1)
        write_x(1)
        arrived(q_in.at[0], Q_IN)
        residue = y_own[0].astype(jnp.float32) - total_of(q_in.at[0])
        arrived(q_in.at[1], Q_IN + 1)
        residue = residue - total_of(q_in.at[1])
        x_own[0] = exact_dot(residue, dinv[0], NN).astype(jnp.bfloat16)
        to_plane(x_own.at[0], x_all.at[0, c], 10, X_ALL)
        write_x(0)
        for index in (1, 2):
            factor_sent(index)
        sent(2, 8, own_column(0))
        sent(3, 4, kq == k)
        sent(5, 15, False)
        sent(6, 4, kq == k)
        sent(7, 15, False)
        sent(8, 8, False)
        sent(9, 8, own_column(0))
        sent(10, 15, False)

    @pl.when(h == 1)
    def _():
        gather(0)
        gathered(0)
        for index in range(1, 4):
            gather(index)
        factor_ready(0)
        arrived(y_in.at[0], Y_IN)
        for kk in range(2):
            put_p(0, kk, product(0, kk, 0))
        to_owner(0, 1)
        solve_forward(0)
        to_column(y_own.at[0], 1, 0, 2)
        sent(2, 8, False)
        to_column(y_own.at[0], 1, 1, 3)
        to_plane(y_own.at[0], y_all.at[0, c], 4, Y_ALL)
        for index in range(1, 4):
            gathered(index)
        factor_ready(1)
        for kk in range(2):
            acc[kk] = product(0, kk, 1)
        factor_ready(2)
        arrived(y_in.at[1], Y_IN + 1)
        for kk in range(2):
            acc[kk] += product(1, kk, 2)
        write_y(0)
        factor_ready(3)
        arrived(y_in.at[2], Y_IN + 2)
        for kk in range(2):
            put_p(1, kk, acc[kk] + product(2, kk, 3))
        to_owner(1, 5)
        solve_forward(1)
        x_own[1] = exact_dot(y_own[1].astype(jnp.float32), dinv[1], NN).astype(jnp.bfloat16)
        to_line(x_own.at[1], 1, 6)
        arrived(x_in.at[1], X_IN + 1)
        for line in range(4):
            put_q(0, line, back_product(1, 3, line))
        to_supernode(0, 2, 0, 9)
        for line in range(4):
            put_q(1, line, back_product(1, 2, line))
        to_supernode(1, 0, 1, 10)
        for line in range(4):
            q_acc[line] = back_product(1, 1, line)
        to_plane(y_own.at[1], y_all.at[1, c], 8, Y_ALL + 1)
        to_plane(x_own.at[1], x_all.at[1, c], 7, X_ALL + 1)
        write_y(1)
        write_x(1)
        arrived(q_in.at[0], Q_IN)
        residue = y_own[0].astype(jnp.float32) - total_of(q_in.at[0])
        arrived(q_in.at[1], Q_IN + 1)
        residue = residue - total_of(q_in.at[1])
        x_own[0] = exact_dot(residue, dinv[0], NN).astype(jnp.bfloat16)
        to_line(x_own.at[0], 0, 11)
        arrived(x_in.at[0], X_IN)
        for line in range(4):
            put_q(2, line, q_acc[line] + back_product(0, 0, line))
        to_supernode(2, 1, 0, 13)
        to_plane(x_own.at[0], x_all.at[0, c], 12, X_ALL)
        write_x(0)
        for index in range(4):
            factor_sent(index)
        sent(1, 4, kq == k)
        sent(3, 8, own_column(1))
        sent(4, 15, False)
        sent(5, 4, kq == k)
        sent(6, 4, kq == k)
        sent(7, 15, False)
        sent(8, 15, False)
        sent(9, 8, False)
        sent(10, 8, own_column(1))
        sent(11, 4, kq == k)
        sent(12, 15, False)
        sent(13, 8, False)


def per_device(factor, pattern, dinv, rhs):
    bf16, f32 = jnp.bfloat16, jnp.float32
    vmem = pl.BlockSpec(memory_space=pltpu.VMEM)
    out = jax.ShapeDtypeStruct((2, 256, 256), bf16)
    forward, back = pl.pallas_call(
        kernel,
        out_shape=(out, out),
        in_specs=[pl.BlockSpec(memory_space=pltpu.HBM)] * 4,
        out_specs=(vmem, vmem),
        scratch_shapes=[
            pltpu.SMEM((2, 4), jnp.int32),
            pltpu.VMEM((4, 256, 256), bf16),
            pltpu.VMEM((2, 256, 256), bf16),
            pltpu.VMEM((2, 256, 256), f32),
            pltpu.VMEM((2, 4, 4, 256, 256), bf16),
            pltpu.VMEM((2, 16, 256), f32),
            pltpu.VMEM((2, 16, 256), bf16),
            pltpu.VMEM((2, 16, 256), bf16),
            pltpu.VMEM((3, 4, 2, 16, 256), bf16),
            pltpu.VMEM((2, 2, 2, 16, 256), bf16),
            pltpu.VMEM((2, 4, 16, 256), bf16),
            pltpu.VMEM((2, 32, 256), f32),
            pltpu.VMEM((2, 16, 16, 256), bf16),
            pltpu.VMEM((2, 2, 2, 16, 256), bf16),
            pltpu.VMEM((2, 16, 16, 256), bf16),
            pltpu.VMEM((256, 256), f32),
            pltpu.VMEM((4, 32, 256), f32),
            pltpu.VMEM((3, 4, 2, 16, 256), bf16),
            pltpu.VMEM((3, 8, 16, 256), bf16),
            pltpu.SemaphoreType.DMA((22,)),
            pltpu.SemaphoreType.DMA((22,)),
            pltpu.SemaphoreType.DMA((7,)),
        ],
        compiler_params=pltpu.CompilerParams(
            collective_id=0, has_side_effects=True, vmem_limit_bytes=60 * 1024 * 1024
        ),
        cost_estimate=pl.CostEstimate(flops=600_000_000, bytes_accessed=3_000_000, transcendentals=0),
    )(pattern[:, 0, :, 0], factor[:, 0, :, 0], dinv[:, 0], rhs[:, 0])
    return forward[:, None], back[:, None]


def solution(mesh):
    placed = (
        P(None, "row", None, "col", None, None),
        P(None, "row", None, "col"),
        P(None, "row", None, None),
        P(None, "row", None, None),
    )
    return jax.shard_map(
        per_device,
        mesh=mesh,
        in_specs=placed,
        out_specs=(P(None, "row", None, None), P(None, "row", None, None)),
        check_vma=False,
    )
```

```python
import jax
import jax.numpy as jnp
from jax import lax
from jax.experimental import pallas as pl
from jax.experimental.pallas import tpu as pltpu
from jax.sharding import PartitionSpec as P

MESH = pl.DeviceIdType.MESH
NT = (((1,), (1,)), ((), ()))
NN = (((1,), (0,)), ((), ()))
PLACES = ((0, 0), (1, 0), (1, 1), (1, 2))
Y_IN, P_IN, Y_ALL, X_IN, X_ALL, Q_IN, L_IN, G_IN, D_IN, B_IN, Y0_IN = 0, 3, 5, 7, 9, 11, 14, 18, 22, 23, 24


def exact_dot(lhs, inverse, dims):
    rows = lhs.shape[0]
    high = lhs.astype(jnp.bfloat16)
    rest = lhs - high.astype(jnp.float32)
    mid = rest.astype(jnp.bfloat16)
    low = (rest - mid.astype(jnp.float32)).astype(jnp.bfloat16)
    stacked = jnp.concatenate([high, mid, low], axis=0)
    out = lax.dot_general(stacked, inverse, dims, preferred_element_type=jnp.float32)
    return out[:rows] + (out[rows : 2 * rows] + out[2 * rows :])


def kernel(
    pattern_hbm, factor_hbm, dinv_hbm, rhs_hbm, out,
    pattern, factor, dinv, rhs, blocks, d_own, b_t, b_own, y_0, y_own, x_own, y_in, p_out, p_in, acc,
    full, x_in, turned, q_acc, q_out, q_in,
    send_sem, recv_sem, load_sem,
):
    r, c = lax.axis_index("row"), lax.axis_index("col")
    z, k = r // 2, r % 2
    h = z // 8
    s = r % 16
    x, y = c // 4, c % 4
    own = y // 2 == z % 2
    core_own = y % 2
    line_own = z % 8 // 2
    source = own & (k == core_own)
    barrier = pltpu.get_barrier_semaphore()
    loads = [
        pltpu.make_async_copy(source, target, load_sem.at[i])
        for i, (source, target) in enumerate(
            ((rhs_hbm, rhs), (dinv_hbm, dinv), (pattern_hbm, pattern))
            + tuple((factor_hbm.at[slot, level], factor.at[j]) for j, (slot, level) in enumerate(PLACES))
        )
    ]
    for load in loads:
        load.start()

    def signal(row, col):
        pl.semaphore_signal(barrier, inc=1, device_id=(row, col), device_id_type=MESH)

    @pl.loop(1, 32)
    def _(p):
        signal((r + p) % 32, c)

    @pl.loop(1, 16)
    def _(p):
        signal(r, (c + p) % 16)
        signal(2 * z + 1 - k, (c + p) % 16)

    def remote(src, dst, event, cls, row, col):
        return pltpu.make_async_remote_copy(
            src_ref=src, dst_ref=dst, send_sem=send_sem.at[event], recv_sem=recv_sem.at[cls],
            device_id=(row, col), device_id_type=MESH,
        )

    def send(src, dst, event, cls, row, col, here):
        @pl.when(here)
        def _():
            pltpu.make_async_copy(src, dst, recv_sem.at[cls]).start()

        @pl.when(jnp.logical_not(here))
        def _():
            remote(src, dst, event, cls, row, col).start()

    def arrived(buf, cls):
        remote(buf, buf, 0, cls, r, c).wait_recv()

    def sent(event, count):
        d = full.at[pl.ds(0, count)]
        remote(d, d, event, 0, r, c).wait_send()

    def sent_unless(here, event, count):
        @pl.when(here)
        def _():
            sent(event, count - 1)

        @pl.when(jnp.logical_not(here))
        def _():
            sent(event, count)

    def to_column(slot, level, half, event):
        def go(p, here):
            args = (y_own.at[slot], y_in.at[level, line_own], event, Y_IN + level,
                    2 * (8 * half + (z + p) % 8) + k, c)
            if here is None:
                remote(*args).start()
            else:
                send(*args, here)

        go(0, half == h)

        @pl.loop(1, 8)
        def _(p):
            go(p, None)

    def first_to_column(half, event):
        def go(p, core, here):
            args = (y_0.at[core], y_in.at[0, line_own], event, Y_IN,
                    2 * (8 * half + (z + p) % 8) + core, c)
            if here is None:
                remote(*args).start()
            else:
                send(*args, here)

        for core in range(2):
            go(0, core, (half == h) & (core == k))

        @pl.loop(1, 8)
        def _(p):
            for core in range(2):
                go(p, core, None)

    def to_owner(slot, event):
        for kk in range(2):
            send(p_out.at[slot, kk], p_in.at[slot, y], event, P_IN + slot, r, 4 * x + 2 * (z % 2) + kk,
                 own & (kk == core_own))

    def to_line(slot, event):
        pltpu.make_async_copy(x_own.at[slot], x_in.at[slot, core_own], recv_sem.at[X_IN + slot]).start()
        for p in range(1, 4):
            remote(x_own.at[slot], x_in.at[slot, core_own], event, X_IN + slot, r, 4 * x + (y + p) % 4).start()

    def to_plane(src, slot, event, cls):
        dst = full.at[8 * slot + 2 * x + k]
        row = 2 * z + core_own
        send(src, dst, event, cls, row, c, source)

        @pl.loop(1, 16)
        def _(p):
            remote(src, dst, event, cls, row, (c + p) % 16).start()

    def to_supernode(slot, cls, half, event):
        for p in range(4):
            line = (line_own + p) % 4
            args = (q_out.at[slot, line], q_in.at[cls, z % 8], event, Q_IN + cls,
                    2 * (8 * half + 2 * line + y // 2) + k, c)
            if p == 0:
                send(*args, own & (half == h))
            else:
                remote(*args).start()

    def share(core, start):
        pairs = [(dinv, d_own, D_IN), (b_t.at[core], b_own, B_IN)]
        for i, (src, dst, cls) in enumerate(pairs):
            if start:
                send(src, dst, 22 + i, cls, 2 * z + core, c, core == k)
            else:
                pl.when(core != k)(remote(src, dst, 22 + i, cls, 2 * z + core, c).wait_send)

    def gather(index):
        for p in range(1, 4):
            block = blocks.at[k, index, x]
            remote(block, block, 14 + index, G_IN + index, r, 4 * ((x + p) % 4) + y).start()

    def swap(index):
        return remote(blocks.at[k, index], blocks.at[k, index], 18 + index, L_IN + index, 2 * z + 1 - k, c)

    def gathered(index):
        arrived(blocks.at[k, index, pl.ds(0, 3)], G_IN + index)
        swap(index).start()

    def factor_ready(index):
        arrived(blocks.at[1 - k, index], L_IN + index)

    def factor_sent(index):
        d = blocks.at[k, index, pl.ds(0, 3)]
        remote(d, d, 14 + index, 0, r, c).wait_send()
        swap(index).wait_send()

    def product(level, kk, index):
        total = None
        for line in range(4):
            term = lax.dot_general(
                y_in[level, line], blocks[kk, index, line], NT,
                preferred_element_type=jnp.float32,
            )
            total = term if total is None else total + term
        return total

    def back_product(slot, index, line):
        total = None
        for kk in range(2):
            term = lax.dot_general(
                x_in[slot, kk], blocks[kk, index, line], NN,
                preferred_element_type=jnp.float32,
            )
            total = term if total is None else total + term
        return total

    def solve_forward(slot):
        arrived(p_in.at[slot], P_IN + slot)
        total = jnp.sum(p_in[slot].astype(jnp.float32), axis=0)
        y_own[slot] = exact_dot(b_own[slot] - total, d_own[slot], NT).astype(jnp.bfloat16)

    def back_total(cls):
        arrived(q_in.at[cls], Q_IN + cls)
        return jnp.sum(q_in[cls].astype(jnp.float32), axis=0)

    def solve_back(slot, *classes):
        residue = y_own[slot].astype(jnp.float32)
        for cls in classes:
            residue = residue - back_total(cls)
        x_own[slot] = exact_dot(residue, d_own[slot], NN).astype(jnp.bfloat16)

    def own_ready():
        arrived(d_own, D_IN)
        arrived(b_own, B_IN)

    def put_p(slot, kk, value):
        p_out[slot, kk] = value.astype(jnp.bfloat16)

    def put_q(slot, line, value):
        q_out[slot, line] = value.astype(jnp.bfloat16)

    def natural(slot):
        value = full[pl.ds(8 * slot, 8)].reshape(256, 256)
        return value.astype(jnp.float32).T.astype(jnp.bfloat16)

    def write_y(slot):
        arrived(full.at[pl.ds(8 * slot, 8)], Y_ALL + slot)
        out[0, slot] = natural(slot)

    def write_x(slot):
        arrived(full.at[pl.ds(16 + 8 * slot, 8)], X_ALL + slot)
        out[1, slot] = natural(2 + slot)

    loads[0].wait()
    for slot in range(2):
        turned[...] = rhs[slot].T
        for core in range(2):
            b_t[core, slot] = turned[pl.ds(pl.multiple_of(64 * x + 32 * core, 32), 32), :]

    loads[1].wait()

    @pl.when(h == 0)
    def _():
        for core in range(2):
            y_0[core] = exact_dot(b_t[core, 0], dinv[0], NT).astype(jnp.bfloat16)

    for load in loads[2:]:
        load.wait()
    for index, (slot, level) in enumerate(PLACES):
        weight = pattern[slot, level].astype(jnp.float32)
        blocks[k, index, x] = (factor[index].astype(jnp.float32) * weight).astype(jnp.bfloat16)

    pl.semaphore_wait(barrier, 61)

    @pl.when(h == 0)
    def _():
        @pl.when(source)
        def _():
            first_to_column(1, 1)
            for core in range(2):
                share(core, True)
                send(y_0.at[core], y_own.at[0], 0, Y0_IN, 2 * z + core, c, core == k)

        gather(1)
        gather(2)
        out[0, 0] = exact_dot(rhs[0].T, dinv[0], NT).T.astype(jnp.bfloat16)
        gathered(1)

        @pl.when(source)
        def _():
            sent(1, 16)
            first_to_column(0, 2)

        gathered(2)
        factor_ready(1)
        arrived(y_in.at[0], Y_IN)
        for kk in range(2):
            acc[kk] = product(0, kk, 1)
        factor_ready(2)
        arrived(y_in.at[1], Y_IN + 1)
        for kk in range(2):
            put_p(1, kk, acc[kk] + product(1, kk, 2))
        to_owner(1, 3)

        @pl.when(own)
        def _():
            own_ready()
            arrived(y_own.at[0], Y0_IN)
            solve_forward(1)
            to_column(1, 2, 1, 4)
            sent(4, 8)
            to_plane(y_own.at[1], 1, 5, Y_ALL + 1)

        write_y(1)

        @pl.when(own)
        def _():
            solve_back(1, 2)
            to_line(1, 6)

        arrived(x_in.at[1], X_IN + 1)
        for line in range(4):
            put_q(0, line, back_product(1, 2, line))
        to_supernode(0, 1, 1, 8)
        for line in range(4):
            put_q(1, line, back_product(1, 1, line))

        @pl.when(own)
        def _():
            to_plane(x_own.at[1], 3, 7, X_ALL + 1)

        to_supernode(1, 0, 0, 9)
        write_x(1)

        @pl.when(own)
        def _():
            solve_back(0, 0, 1)
            to_plane(x_own.at[0], 2, 10, X_ALL)

        write_x(0)
        for index in (1, 2):
            factor_sent(index)
        sent_unless(own, 3, 2)
        sent(8, 4)
        sent_unless(own, 9, 4)

        @pl.when(source)
        def _():
            sent(2, 15)
            sent(0, 1)
            for core in range(2):
                share(core, False)

        @pl.when(own)
        def _():
            sent_unless(source, 5, 16)
            sent(6, 3)
            sent_unless(source, 7, 16)
            sent_unless(source, 10, 16)

    @pl.when(h == 1)
    def _():
        gather(0)

        @pl.when(source)
        def _():
            for core in range(2):
                share(core, True)

        gathered(0)
        for index in range(1, 4):
            gather(index)
        factor_ready(0)
        arrived(y_in.at[0], Y_IN)
        for kk in range(2):
            put_p(0, kk, product(0, kk, 0))
        to_owner(0, 1)

        @pl.when(own)
        def _():
            own_ready()
            solve_forward(0)
            to_column(0, 1, 0, 2)
            sent(2, 8)
            to_plane(y_own.at[0], 0, 4, Y_ALL)

        for index in range(1, 4):
            gathered(index)
        factor_ready(1)
        for kk in range(2):
            acc[kk] = product(0, kk, 1)
        write_y(0)

        @pl.when(own)
        def _():
            to_column(0, 1, 1, 3)

        factor_ready(2)
        arrived(y_in.at[1], Y_IN + 1)
        for kk in range(2):
            acc[kk] += product(1, kk, 2)
        factor_ready(3)
        arrived(y_in.at[2], Y_IN + 2)
        for kk in range(2):
            put_p(1, kk, acc[kk] + product(2, kk, 3))
        to_owner(1, 5)

        @pl.when(own)
        def _():
            solve_forward(1)
            solve_back(1)
            to_line(1, 6)

        arrived(x_in.at[1], X_IN + 1)
        for line in range(4):
            put_q(0, line, back_product(1, 3, line))
        to_supernode(0, 2, 0, 9)

        @pl.when(own)
        def _():
            to_plane(y_own.at[1], 1, 8, Y_ALL + 1)
            to_plane(x_own.at[1], 3, 7, X_ALL + 1)

        for line in range(4):
            put_q(1, line, back_product(1, 2, line))
        for line in range(4):
            q_acc[line] = back_product(1, 1, line)
        write_y(1)
        to_supernode(1, 0, 1, 10)
        write_x(1)

        @pl.when(own)
        def _():
            solve_back(0, 0, 1)
            to_line(0, 11)

        arrived(x_in.at[0], X_IN)
        for line in range(4):
            put_q(2, line, q_acc[line] + back_product(0, 0, line))
        to_supernode(2, 1, 0, 13)

        @pl.when(own)
        def _():
            to_plane(x_own.at[0], 2, 12, X_ALL)

        write_x(0)
        for index in range(4):
            factor_sent(index)
        sent_unless(own, 1, 2)
        sent_unless(own, 5, 2)
        sent(9, 4)
        sent_unless(own, 10, 4)
        sent(13, 4)

        @pl.when(source)
        def _():
            for core in range(2):
                share(core, False)

        @pl.when(own)
        def _():
            sent(3, 7)
            sent_unless(source, 4, 16)
            sent(6, 3)
            sent_unless(source, 7, 16)
            sent_unless(source, 8, 16)
            sent(11, 3)
            sent_unless(source, 12, 16)


def per_device(factor, pattern, dinv, rhs):
    bf16, f32 = jnp.bfloat16, jnp.float32
    vmem = pl.BlockSpec(memory_space=pltpu.VMEM)
    result = pl.pallas_call(
        kernel,
        out_shape=jax.ShapeDtypeStruct((2, 2, 256, 256), bf16),
        in_specs=[pl.BlockSpec(memory_space=pltpu.HBM)] * 4,
        out_specs=vmem,
        scratch_shapes=[
            pltpu.SMEM((2, 4), jnp.int32),
            pltpu.VMEM((4, 256, 256), bf16),
            pltpu.VMEM((2, 256, 256), bf16),
            pltpu.VMEM((2, 256, 256), f32),
            pltpu.VMEM((2, 4, 4, 256, 256), bf16),
            pltpu.VMEM((2, 256, 256), bf16),
            pltpu.VMEM((2, 2, 32, 256), f32),
            pltpu.VMEM((2, 32, 256), f32),
            pltpu.VMEM((2, 32, 256), bf16),
            pltpu.VMEM((2, 32, 256), bf16),
            pltpu.VMEM((2, 32, 256), bf16),
            pltpu.VMEM((3, 4, 32, 256), bf16),
            pltpu.VMEM((2, 2, 32, 256), bf16),
            pltpu.VMEM((2, 4, 32, 256), bf16),
            pltpu.VMEM((2, 32, 256), f32),
            pltpu.VMEM((32, 32, 256), bf16),
            pltpu.VMEM((2, 2, 32, 256), bf16),
            pltpu.VMEM((256, 256), f32),
            pltpu.VMEM((4, 32, 256), f32),
            pltpu.VMEM((3, 4, 32, 256), bf16),
            pltpu.VMEM((3, 8, 32, 256), bf16),
            pltpu.SemaphoreType.DMA((24,)),
            pltpu.SemaphoreType.DMA((25,)),
            pltpu.SemaphoreType.DMA((7,)),
        ],
        compiler_params=pltpu.CompilerParams(
            collective_id=0, has_side_effects=True, vmem_limit_bytes=60 * 1024 * 1024
        ),
        cost_estimate=pl.CostEstimate(flops=600_000_000, bytes_accessed=3_000_000, transcendentals=0),
    )(pattern[:, 0, :, 0], factor[:, 0, :, 0], dinv[:, 0], rhs[:, 0])
    return result[0][:, None], result[1][:, None]


def solution(mesh):
    placed = (
        P(None, "row", None, "col", None, None),
        P(None, "row", None, "col"),
        P(None, "row", None, None),
        P(None, "row", None, None),
    )
    return jax.shard_map(
        per_device,
        mesh=mesh,
        in_specs=placed,
        out_specs=(P(None, "row", None, None), P(None, "row", None, None)),
        check_vma=False,
    )
```

```python
import jax
import jax.numpy as jnp
from jax import lax
from jax.experimental import pallas as pl
from jax.experimental.pallas import tpu as pltpu
from jax.sharding import PartitionSpec as P

MESH = pl.DeviceIdType.MESH
NT = (((1,), (1,)), ((), ()))
NN = (((1,), (0,)), ((), ()))
PLACES = ((0, 0), (1, 0), (1, 1), (1, 2))
Y_IN, P_IN, Y_ALL, X_IN, X_ALL, Q_IN, L_IN, G_IN, D_IN, B_IN, Y0_IN = 0, 3, 5, 7, 9, 11, 14, 18, 22, 23, 24


def exact_dot(lhs, inverse, dims):
    rows = lhs.shape[0]
    high = lhs.astype(jnp.bfloat16)
    rest = lhs - high.astype(jnp.float32)
    mid = rest.astype(jnp.bfloat16)
    low = (rest - mid.astype(jnp.float32)).astype(jnp.bfloat16)
    stacked = jnp.concatenate([high, mid, low], axis=0)
    out = lax.dot_general(stacked, inverse, dims, preferred_element_type=jnp.float32)
    return out[:rows] + (out[rows : 2 * rows] + out[2 * rows :])


def kernel(
    pattern_hbm, factor_hbm, dinv_hbm, rhs_hbm, out,
    pattern, factor, dinv, rhs, blocks, d_own, b_t, b_own, y_0, y_own, x_own, y_in, p_out, p_in, acc,
    full, x_in, turned, q_acc, q_out, q_in,
    send_sem, recv_sem, load_sem,
):
    r, c = lax.axis_index("row"), lax.axis_index("col")
    z, k = r // 2, r % 2
    h = z // 8
    s = r % 16
    x, y = c // 4, c % 4
    own = y // 2 == z % 2
    core_own = y % 2
    line_own = z % 8 // 2
    source = own & (k == core_own)
    barrier = pltpu.get_barrier_semaphore()
    loads = [
        pltpu.make_async_copy(source, target, load_sem.at[i])
        for i, (source, target) in enumerate(
            ((rhs_hbm, rhs), (dinv_hbm, dinv), (pattern_hbm, pattern))
            + tuple((factor_hbm.at[slot, level], factor.at[j]) for j, (slot, level) in enumerate(PLACES))
        )
    ]
    for load in loads:
        load.start()

    def signal(row, col):
        pl.semaphore_signal(barrier, inc=1, device_id=(row, col), device_id_type=MESH)

    @pl.loop(1, 32)
    def _(p):
        signal((r + p) % 32, c)

    @pl.loop(1, 16)
    def _(p):
        signal(r, (c + p) % 16)
        signal(2 * z + 1 - k, (c + p) % 16)

    def remote(src, dst, event, cls, row, col):
        return pltpu.make_async_remote_copy(
            src_ref=src, dst_ref=dst, send_sem=send_sem.at[event], recv_sem=recv_sem.at[cls],
            device_id=(row, col), device_id_type=MESH,
        )

    def send(src, dst, event, cls, row, col, here):
        @pl.when(here)
        def _():
            pltpu.make_async_copy(src, dst, recv_sem.at[cls]).start()

        @pl.when(jnp.logical_not(here))
        def _():
            remote(src, dst, event, cls, row, col).start()

    def arrived(buf, cls):
        remote(buf, buf, 0, cls, r, c).wait_recv()

    def sent(event, count):
        d = full.at[pl.ds(0, count)]
        remote(d, d, event, 0, r, c).wait_send()

    def sent_unless(here, event, count):
        @pl.when(here)
        def _():
            sent(event, count - 1)

        @pl.when(jnp.logical_not(here))
        def _():
            sent(event, count)

    def to_column(slot, level, half, event):
        def go(p, here):
            args = (y_own.at[slot], y_in.at[level, line_own], event, Y_IN + level,
                    2 * (8 * half + (z + p) % 8) + k, c)
            if here is None:
                remote(*args).start()
            else:
                send(*args, here)

        go(0, half == h)

        @pl.loop(1, 8)
        def _(p):
            go(p, None)

    def first_to_column(half, event):
        def go(p, core, here):
            args = (y_0.at[core], y_in.at[0, line_own], event, Y_IN,
                    2 * (8 * half + (z + p) % 8) + core, c)
            if here is None:
                remote(*args).start()
            else:
                send(*args, here)

        for core in range(2):
            go(0, core, (half == h) & (core == k))

        @pl.loop(1, 8)
        def _(p):
            for core in range(2):
                go(p, core, None)

    def to_owner(slot, event):
        for kk in range(2):
            send(p_out.at[slot, kk], p_in.at[slot, y], event, P_IN + slot, r, 4 * x + 2 * (z % 2) + kk,
                 own & (kk == core_own))

    def to_line(slot, event):
        pltpu.make_async_copy(x_own.at[slot], x_in.at[slot, core_own], recv_sem.at[X_IN + slot]).start()
        for p in range(1, 4):
            remote(x_own.at[slot], x_in.at[slot, core_own], event, X_IN + slot, r, 4 * x + (y + p) % 4).start()

    def to_plane(src, slot, event, cls):
        dst = full.at[8 * slot + 2 * x + k]
        row = 2 * z + core_own
        send(src, dst, event, cls, row, c, source)

        @pl.loop(1, 16)
        def _(p):
            remote(src, dst, event, cls, row, (c + p) % 16).start()

    def to_lines(slot, event):
        for p in range(4):
            for core in range(2):
                args = (x_in.at[slot, core], full.at[16 + 8 * slot + 2 * x + k], event, X_ALL + slot,
                        2 * z + core, 4 * ((x + p) % 4) + y)
                if p == 0:
                    send(*args, core == k)
                else:
                    remote(*args).start()

    def to_supernode(slot, cls, half, event):
        for p in range(4):
            line = (line_own + p) % 4
            args = (q_out.at[slot, line], q_in.at[cls, z % 8], event, Q_IN + cls,
                    2 * (8 * half + 2 * line + y // 2) + k, c)
            if p == 0:
                send(*args, own & (half == h))
            else:
                remote(*args).start()

    def share(core, start):
        pairs = [(dinv, d_own, D_IN), (b_t.at[core], b_own, B_IN)]
        for i, (src, dst, cls) in enumerate(pairs):
            if start:
                send(src, dst, 22 + i, cls, 2 * z + core, c, core == k)
            else:
                pl.when(core != k)(remote(src, dst, 22 + i, cls, 2 * z + core, c).wait_send)

    def gather(index):
        for p in range(1, 4):
            block = blocks.at[k, index, x]
            remote(block, block, 14 + index, G_IN + index, r, 4 * ((x + p) % 4) + y).start()

    def swap(index):
        return remote(blocks.at[k, index], blocks.at[k, index], 18 + index, L_IN + index, 2 * z + 1 - k, c)

    def gathered(index):
        arrived(blocks.at[k, index, pl.ds(0, 3)], G_IN + index)
        swap(index).start()

    def factor_ready(index):
        arrived(blocks.at[1 - k, index], L_IN + index)

    def factor_sent(index):
        d = blocks.at[k, index, pl.ds(0, 3)]
        remote(d, d, 14 + index, 0, r, c).wait_send()
        swap(index).wait_send()

    def product(level, kk, index):
        total = None
        for line in range(4):
            term = lax.dot_general(
                y_in[level, line], blocks[kk, index, line], NT,
                preferred_element_type=jnp.float32,
            )
            total = term if total is None else total + term
        return total

    def back_product(slot, index, line):
        total = None
        for kk in range(2):
            term = lax.dot_general(
                x_in[slot, kk], blocks[kk, index, line], NN,
                preferred_element_type=jnp.float32,
            )
            total = term if total is None else total + term
        return total

    def solve_forward(slot):
        arrived(p_in.at[slot], P_IN + slot)
        total = jnp.sum(p_in[slot].astype(jnp.float32), axis=0)
        y_own[slot] = exact_dot(b_own[slot] - total, d_own[slot], NT).astype(jnp.bfloat16)

    def back_total(cls):
        arrived(q_in.at[cls], Q_IN + cls)
        return jnp.sum(q_in[cls].astype(jnp.float32), axis=0)

    def solve_back(slot, *classes):
        residue = y_own[slot].astype(jnp.float32)
        for cls in classes:
            residue = residue - back_total(cls)
        x_own[slot] = exact_dot(residue, d_own[slot], NN).astype(jnp.bfloat16)

    def own_ready():
        arrived(d_own, D_IN)
        arrived(b_own, B_IN)

    def put_p(slot, kk, value):
        p_out[slot, kk] = value.astype(jnp.bfloat16)

    def put_q(slot, line, value):
        q_out[slot, line] = value.astype(jnp.bfloat16)

    def natural(slot):
        value = full[pl.ds(8 * slot, 8)].reshape(256, 256)
        return value.astype(jnp.float32).T.astype(jnp.bfloat16)

    def write_y(slot):
        arrived(full.at[pl.ds(8 * slot, 8)], Y_ALL + slot)
        out[0, slot] = natural(slot)

    def write_x(slot):
        arrived(full.at[pl.ds(16 + 8 * slot, 8)], X_ALL + slot)
        out[1, slot] = natural(2 + slot)

    loads[0].wait()
    for slot in range(2):
        turned[...] = rhs[slot].T
        for core in range(2):
            b_t[core, slot] = turned[pl.ds(pl.multiple_of(64 * x + 32 * core, 32), 32), :]

    loads[1].wait()

    @pl.when(h == 0)
    def _():
        for core in range(2):
            y_0[core] = exact_dot(b_t[core, 0], dinv[0], NT).astype(jnp.bfloat16)

    for load in loads[2:]:
        load.wait()
    for index, (slot, level) in enumerate(PLACES):
        weight = pattern[slot, level].astype(jnp.float32)
        blocks[k, index, x] = (factor[index].astype(jnp.float32) * weight).astype(jnp.bfloat16)

    pl.semaphore_wait(barrier, 61)

    @pl.when(h == 0)
    def _():
        @pl.when(source)
        def _():
            first_to_column(1, 1)
            for core in range(2):
                share(core, True)
                send(y_0.at[core], y_own.at[0], 0, Y0_IN, 2 * z + core, c, core == k)
            sent(1, 16)
            first_to_column(0, 2)

        gather(1)
        gather(2)
        out[0, 0] = exact_dot(rhs[0].T, dinv[0], NT).T.astype(jnp.bfloat16)
        gathered(1)
        gathered(2)
        factor_ready(1)
        arrived(y_in.at[0], Y_IN)
        for kk in range(2):
            acc[kk] = product(0, kk, 1)
        factor_ready(2)
        arrived(y_in.at[1], Y_IN + 1)
        for kk in range(2):
            put_p(1, kk, acc[kk] + product(1, kk, 2))
        to_owner(1, 3)

        @pl.when(own)
        def _():
            own_ready()
            arrived(y_own.at[0], Y0_IN)
            solve_forward(1)
            to_column(1, 2, 1, 4)
            sent(4, 8)
            to_plane(y_own.at[1], 1, 5, Y_ALL + 1)

        write_y(1)

        @pl.when(own)
        def _():
            solve_back(1, 2)
            to_line(1, 6)

        arrived(x_in.at[1], X_IN + 1)
        for line in range(4):
            put_q(0, line, back_product(1, 2, line))
        to_supernode(0, 1, 1, 8)
        for line in range(4):
            put_q(1, line, back_product(1, 1, line))

        to_lines(1, 7)
        to_supernode(1, 0, 0, 9)
        write_x(1)

        @pl.when(own)
        def _():
            solve_back(0, 0, 1)
            to_plane(x_own.at[0], 2, 10, X_ALL)

        write_x(0)
        for index in (1, 2):
            factor_sent(index)
        sent_unless(own, 3, 2)
        sent(8, 4)
        sent(7, 7)
        sent_unless(own, 9, 4)

        @pl.when(source)
        def _():
            sent(2, 15)
            sent(0, 1)
            for core in range(2):
                share(core, False)

        @pl.when(own)
        def _():
            sent_unless(source, 5, 16)
            sent(6, 3)
            sent_unless(source, 10, 16)

    @pl.when(h == 1)
    def _():
        gather(0)

        @pl.when(source)
        def _():
            for core in range(2):
                share(core, True)

        gathered(0)
        for index in range(1, 4):
            gather(index)
        factor_ready(0)
        arrived(y_in.at[0], Y_IN)
        for kk in range(2):
            put_p(0, kk, product(0, kk, 0))
        to_owner(0, 1)

        @pl.when(own)
        def _():
            own_ready()
            solve_forward(0)
            to_column(0, 1, 0, 2)
            sent(2, 8)
            to_column(0, 1, 1, 3)

        for index in range(1, 4):
            gathered(index)
        factor_ready(1)
        for kk in range(2):
            acc[kk] = product(0, kk, 1)

        @pl.when(own)
        def _():
            to_plane(y_own.at[0], 0, 4, Y_ALL)

        factor_ready(2)
        arrived(y_in.at[1], Y_IN + 1)
        for kk in range(2):
            acc[kk] += product(1, kk, 2)
        write_y(0)
        factor_ready(3)
        arrived(y_in.at[2], Y_IN + 2)
        for kk in range(2):
            put_p(1, kk, acc[kk] + product(2, kk, 3))
        to_owner(1, 5)

        @pl.when(own)
        def _():
            solve_forward(1)
            solve_back(1)
            to_line(1, 6)

        arrived(x_in.at[1], X_IN + 1)
        for line in range(4):
            put_q(0, line, back_product(1, 3, line))
        to_supernode(0, 2, 0, 9)
        to_lines(1, 7)

        @pl.when(own)
        def _():
            to_plane(y_own.at[1], 1, 8, Y_ALL + 1)

        for line in range(4):
            put_q(1, line, back_product(1, 2, line))
        for line in range(4):
            q_acc[line] = back_product(1, 1, line)
        write_y(1)
        to_supernode(1, 0, 1, 10)
        write_x(1)

        @pl.when(own)
        def _():
            solve_back(0, 0, 1)
            to_line(0, 11)

        arrived(x_in.at[0], X_IN)
        for line in range(4):
            put_q(2, line, q_acc[line] + back_product(0, 0, line))
        to_supernode(2, 1, 0, 13)

        to_lines(0, 12)
        write_x(0)
        for index in range(4):
            factor_sent(index)
        sent_unless(own, 1, 2)
        sent_unless(own, 5, 2)
        sent(9, 4)
        sent(7, 7)
        sent(12, 7)
        sent_unless(own, 10, 4)
        sent(13, 4)

        @pl.when(source)
        def _():
            for core in range(2):
                share(core, False)

        @pl.when(own)
        def _():
            sent(3, 7)
            sent_unless(source, 4, 16)
            sent(6, 3)
            sent_unless(source, 8, 16)
            sent(11, 3)


def per_device(factor, pattern, dinv, rhs):
    bf16, f32 = jnp.bfloat16, jnp.float32
    vmem = pl.BlockSpec(memory_space=pltpu.VMEM)
    result = pl.pallas_call(
        kernel,
        out_shape=jax.ShapeDtypeStruct((2, 2, 256, 256), bf16),
        in_specs=[pl.BlockSpec(memory_space=pltpu.HBM)] * 4,
        out_specs=vmem,
        scratch_shapes=[
            pltpu.SMEM((2, 4), jnp.int32),
            pltpu.VMEM((4, 256, 256), bf16),
            pltpu.VMEM((2, 256, 256), bf16),
            pltpu.VMEM((2, 256, 256), f32),
            pltpu.VMEM((2, 4, 4, 256, 256), bf16),
            pltpu.VMEM((2, 256, 256), bf16),
            pltpu.VMEM((2, 2, 32, 256), f32),
            pltpu.VMEM((2, 32, 256), f32),
            pltpu.VMEM((2, 32, 256), bf16),
            pltpu.VMEM((2, 32, 256), bf16),
            pltpu.VMEM((2, 32, 256), bf16),
            pltpu.VMEM((3, 4, 32, 256), bf16),
            pltpu.VMEM((2, 2, 32, 256), bf16),
            pltpu.VMEM((2, 4, 32, 256), bf16),
            pltpu.VMEM((2, 32, 256), f32),
            pltpu.VMEM((32, 32, 256), bf16),
            pltpu.VMEM((2, 2, 32, 256), bf16),
            pltpu.VMEM((256, 256), f32),
            pltpu.VMEM((4, 32, 256), f32),
            pltpu.VMEM((3, 4, 32, 256), bf16),
            pltpu.VMEM((3, 8, 32, 256), bf16),
            pltpu.SemaphoreType.DMA((24,)),
            pltpu.SemaphoreType.DMA((25,)),
            pltpu.SemaphoreType.DMA((7,)),
        ],
        compiler_params=pltpu.CompilerParams(
            collective_id=0, has_side_effects=True, vmem_limit_bytes=60 * 1024 * 1024
        ),
        cost_estimate=pl.CostEstimate(flops=600_000_000, bytes_accessed=3_000_000, transcendentals=0),
    )(pattern[:, 0, :, 0], factor[:, 0, :, 0], dinv[:, 0], rhs[:, 0])
    return result[0][:, None], result[1][:, None]


def solution(mesh):
    placed = (
        P(None, "row", None, "col", None, None),
        P(None, "row", None, "col"),
        P(None, "row", None, None),
        P(None, "row", None, None),
    )
    return jax.shard_map(
        per_device,
        mesh=mesh,
        in_specs=placed,
        out_specs=(P(None, "row", None, None), P(None, "row", None, None)),
        check_vma=False,
    )
```

```python
import jax
import jax.numpy as jnp
from jax import lax
from jax.experimental import pallas as pl
from jax.experimental.pallas import tpu as pltpu
from jax.sharding import PartitionSpec as P

MESH = pl.DeviceIdType.MESH
NT = (((1,), (1,)), ((), ()))
NN = (((1,), (0,)), ((), ()))
PLACES = ((0, 0), (1, 0), (1, 1), (1, 2))
Y_IN, P_IN, Y_ALL, X_IN, X_ALL, Q_IN, L_IN, G_IN, D_IN, B_IN, Y0_IN, G_0 = 0, 3, 5, 7, 9, 11, 14, 18, 22, 23, 24, 25


def exact_dot(lhs, inverse, dims):
    rows = lhs.shape[0]
    high = lhs.astype(jnp.bfloat16)
    rest = lhs - high.astype(jnp.float32)
    mid = rest.astype(jnp.bfloat16)
    low = (rest - mid.astype(jnp.float32)).astype(jnp.bfloat16)
    stacked = jnp.concatenate([high, mid, low], axis=0)
    out = lax.dot_general(stacked, inverse, dims, preferred_element_type=jnp.float32)
    return out[:rows] + (out[rows : 2 * rows] + out[2 * rows :])


def kernel(
    pattern_hbm, factor_hbm, dinv_hbm, rhs_hbm, out,
    pattern, factor, dinv, rhs, blocks, d_own, b_t, b_own, y_0, y_own, x_own, y_in, p_out, p_in, acc,
    full, x_in, turned, q_acc, q_out, q_in,
    send_sem, recv_sem, load_sem,
):
    r, c = lax.axis_index("row"), lax.axis_index("col")
    z, k = r // 2, r % 2
    h = z // 8
    s = r % 16
    x, y = c // 4, c % 4
    own = y // 2 == z % 2
    core_own = y % 2
    line_own = z % 8 // 2
    source = own & (k == core_own)
    barrier = pltpu.get_barrier_semaphore()
    loads = [
        pltpu.make_async_copy(source, target, load_sem.at[i])
        for i, (source, target) in enumerate(
            ((rhs_hbm, rhs), (dinv_hbm, dinv), (pattern_hbm, pattern))
            + tuple((factor_hbm.at[slot, level], factor.at[j]) for j, (slot, level) in enumerate(PLACES))
        )
    ]
    for load in loads:
        load.start()

    def signal(row, col):
        pl.semaphore_signal(barrier, inc=1, device_id=(row, col), device_id_type=MESH)

    @pl.loop(1, 32)
    def _(p):
        signal((r + p) % 32, c)

    @pl.loop(1, 16)
    def _(p):
        signal(r, (c + p) % 16)
        signal(2 * z + 1 - k, (c + p) % 16)

    def remote(src, dst, event, cls, row, col):
        return pltpu.make_async_remote_copy(
            src_ref=src, dst_ref=dst, send_sem=send_sem.at[event], recv_sem=recv_sem.at[cls],
            device_id=(row, col), device_id_type=MESH,
        )

    def send(src, dst, event, cls, row, col, here):
        @pl.when(here)
        def _():
            pltpu.make_async_copy(src, dst, recv_sem.at[cls]).start()

        @pl.when(jnp.logical_not(here))
        def _():
            remote(src, dst, event, cls, row, col).start()

    def arrived(buf, cls):
        remote(buf, buf, 0, cls, r, c).wait_recv()

    def sent(event, count):
        d = full.at[pl.ds(0, count)]
        remote(d, d, event, 0, r, c).wait_send()

    def sent_unless(here, event, count):
        @pl.when(here)
        def _():
            sent(event, count - 1)

        @pl.when(jnp.logical_not(here))
        def _():
            sent(event, count)

    def to_column(slot, level, half, event):
        def go(p, here):
            args = (y_own.at[slot], y_in.at[level, line_own], event, Y_IN + level,
                    2 * (8 * half + (z + p) % 8) + k, c)
            if here is None:
                remote(*args).start()
            else:
                send(*args, here)

        go(0, half == h)

        @pl.loop(1, 8)
        def _(p):
            go(p, None)

    def first_to_column(half, event):
        def go(p, core, here):
            args = (y_0.at[core], y_in.at[0, line_own], event, Y_IN,
                    2 * (8 * half + (z + p) % 8) + core, c)
            if here is None:
                remote(*args).start()
            else:
                send(*args, here)

        for core in range(2):
            go(0, core, (half == h) & (core == k))

        @pl.loop(1, 8)
        def _(p):
            for core in range(2):
                go(p, core, None)

    def to_owner(slot, event):
        for kk in range(2):
            send(p_out.at[slot, kk], p_in.at[slot, y], event, P_IN + slot, r, 4 * x + 2 * (z % 2) + kk,
                 own & (kk == core_own))

    def to_line(slot, event):
        pltpu.make_async_copy(x_own.at[slot], x_in.at[slot, core_own], recv_sem.at[X_IN + slot]).start()
        for p in range(1, 4):
            remote(x_own.at[slot], x_in.at[slot, core_own], event, X_IN + slot, r, 4 * x + (y + p) % 4).start()

    def to_plane(src, slot, event, cls):
        dst = full.at[8 * slot + 2 * x + k]
        row = 2 * z + core_own
        send(src, dst, event, cls, row, c, source)

        @pl.loop(1, 16)
        def _(p):
            remote(src, dst, event, cls, row, (c + p) % 16).start()

    def to_lines(slot, event):
        for p in range(4):
            for core in range(2):
                args = (x_in.at[slot, core], full.at[16 + 8 * slot + 2 * x + k], event, X_ALL + slot,
                        2 * z + core, 4 * ((x + p) % 4) + y)
                if p == 0:
                    send(*args, core == k)
                else:
                    remote(*args).start()

    def to_supernode(slot, cls, half, event):
        for p in range(4):
            line = (line_own + p) % 4
            args = (q_out.at[slot, line], q_in.at[cls, z % 8], event, Q_IN + cls,
                    2 * (8 * half + 2 * line + y // 2) + k, c)
            if p == 0:
                send(*args, own & (half == h))
            else:
                remote(*args).start()

    def share(core, start):
        pairs = [(dinv, d_own, D_IN), (b_t.at[core], b_own, B_IN)]
        for i, (src, dst, cls) in enumerate(pairs):
            if start:
                send(src, dst, 22 + i, cls, 2 * z + core, c, core == k)
            else:
                pl.when(core != k)(remote(src, dst, 22 + i, cls, 2 * z + core, c).wait_send)

    def gather(index):
        block = blocks.at[k, index, x]
        for p in (2, 1, 3):
            cls = G_0 + p - 1 if index == 0 else G_IN + index
            remote(block, block, 14 + index, cls, r, 4 * ((x + p) % 4) + y).start()
        swap(index, x).start()

    def swap(index, line):
        block = blocks.at[k, index, line]
        return remote(block, block, 18 + index, L_IN + index, 2 * z + 1 - k, c)

    def gathered(index):
        if index > 0:
            arrived(blocks.at[k, index, pl.ds(0, 3)], G_IN + index)
        for p in (1, 3, 2):
            line = (x + 4 - p) % 4
            if index == 0:
                arrived(blocks.at[k, index, line], G_0 + p - 1)
            swap(index, line).start()

    def factor_ready(index):
        arrived(blocks.at[1 - k, index], L_IN + index)

    def factor_sent(index):
        d = blocks.at[k, index, pl.ds(0, 3)]
        remote(d, d, 14 + index, 0, r, c).wait_send()
        d = blocks.at[k, index]
        remote(d, d, 18 + index, 0, r, c).wait_send()

    def product(level, kk, index):
        total = None
        for line in range(4):
            term = lax.dot_general(
                y_in[level, line], blocks[kk, index, line], NT,
                preferred_element_type=jnp.float32,
            )
            total = term if total is None else total + term
        return total

    def back_product(slot, index, line):
        total = None
        for kk in range(2):
            term = lax.dot_general(
                x_in[slot, kk], blocks[kk, index, line], NN,
                preferred_element_type=jnp.float32,
            )
            total = term if total is None else total + term
        return total

    def solve_forward(slot):
        arrived(p_in.at[slot], P_IN + slot)
        total = jnp.sum(p_in[slot].astype(jnp.float32), axis=0)
        y_own[slot] = exact_dot(b_own[slot] - total, d_own[slot], NT).astype(jnp.bfloat16)

    def back_total(cls):
        arrived(q_in.at[cls], Q_IN + cls)
        return jnp.sum(q_in[cls].astype(jnp.float32), axis=0)

    def solve_back(slot, *classes):
        residue = y_own[slot].astype(jnp.float32)
        for cls in classes:
            residue = residue - back_total(cls)
        x_own[slot] = exact_dot(residue, d_own[slot], NN).astype(jnp.bfloat16)

    def own_ready():
        arrived(d_own, D_IN)
        arrived(b_own, B_IN)

    def put_p(slot, kk, value):
        p_out[slot, kk] = value.astype(jnp.bfloat16)

    def put_q(slot, line, value):
        q_out[slot, line] = value.astype(jnp.bfloat16)

    def natural(slot):
        value = full[pl.ds(8 * slot, 8)].reshape(256, 256)
        return value.astype(jnp.float32).T.astype(jnp.bfloat16)

    def write_y(slot):
        arrived(full.at[pl.ds(8 * slot, 8)], Y_ALL + slot)
        out[0, slot] = natural(slot)

    def write_x(slot):
        arrived(full.at[pl.ds(16 + 8 * slot, 8)], X_ALL + slot)
        out[1, slot] = natural(2 + slot)

    loads[0].wait()
    for slot in range(2):
        turned[...] = rhs[slot].T
        for core in range(2):
            b_t[core, slot] = turned[pl.ds(pl.multiple_of(64 * x + 32 * core, 32), 32), :]

    loads[1].wait()

    @pl.when(h == 0)
    def _():
        for core in range(2):
            y_0[core] = exact_dot(b_t[core, 0], dinv[0], NT).astype(jnp.bfloat16)

    for load in loads[2:]:
        load.wait()
    for index, (slot, level) in enumerate(PLACES):
        weight = pattern[slot, level].astype(jnp.float32)
        blocks[k, index, x] = (factor[index].astype(jnp.float32) * weight).astype(jnp.bfloat16)

    pl.semaphore_wait(barrier, 61)

    @pl.when(h == 0)
    def _():
        @pl.when(source)
        def _():
            first_to_column(1, 1)
            for core in range(2):
                share(core, True)
                send(y_0.at[core], y_own.at[0], 0, Y0_IN, 2 * z + core, c, core == k)
            sent(1, 16)
            first_to_column(0, 2)

        gather(1)
        gather(2)
        out[0, 0] = exact_dot(rhs[0].T, dinv[0], NT).T.astype(jnp.bfloat16)
        gathered(1)
        gathered(2)
        factor_ready(1)
        arrived(y_in.at[0], Y_IN)
        for kk in range(2):
            acc[kk] = product(0, kk, 1)
        factor_ready(2)
        arrived(y_in.at[1], Y_IN + 1)
        for kk in range(2):
            put_p(1, kk, acc[kk] + product(1, kk, 2))
        to_owner(1, 3)

        @pl.when(own)
        def _():
            own_ready()
            arrived(y_own.at[0], Y0_IN)
            solve_forward(1)
            to_column(1, 2, 1, 4)
            sent(4, 8)
            to_plane(y_own.at[1], 1, 5, Y_ALL + 1)

        write_y(1)

        @pl.when(own)
        def _():
            solve_back(1, 2)
            to_line(1, 6)

        arrived(x_in.at[1], X_IN + 1)
        for line in range(4):
            put_q(0, line, back_product(1, 2, line))
        to_supernode(0, 1, 1, 8)
        for line in range(4):
            put_q(1, line, back_product(1, 1, line))

        to_lines(1, 7)
        to_supernode(1, 0, 0, 9)
        write_x(1)

        @pl.when(own)
        def _():
            solve_back(0, 0, 1)
            to_plane(x_own.at[0], 2, 10, X_ALL)

        write_x(0)
        for index in (1, 2):
            factor_sent(index)
        sent_unless(own, 3, 2)
        sent(8, 4)
        sent(7, 7)
        sent_unless(own, 9, 4)

        @pl.when(source)
        def _():
            sent(2, 15)
            sent(0, 1)
            for core in range(2):
                share(core, False)

        @pl.when(own)
        def _():
            sent_unless(source, 5, 16)
            sent(6, 3)
            sent_unless(source, 10, 16)

    @pl.when(h == 1)
    def _():
        gather(0)

        @pl.when(source)
        def _():
            for core in range(2):
                share(core, True)

        gathered(0)
        for index in range(1, 4):
            gather(index)
        factor_ready(0)
        arrived(y_in.at[0], Y_IN)
        for kk in range(2):
            put_p(0, kk, product(0, kk, 0))
        to_owner(0, 1)

        @pl.when(own)
        def _():
            own_ready()
            solve_forward(0)
            to_column(0, 1, 0, 2)
            sent(2, 8)
            to_column(0, 1, 1, 3)

        for index in range(1, 4):
            gathered(index)
        factor_ready(1)
        for kk in range(2):
            acc[kk] = product(0, kk, 1)

        @pl.when(own)
        def _():
            to_plane(y_own.at[0], 0, 4, Y_ALL)

        factor_ready(2)
        arrived(y_in.at[1], Y_IN + 1)
        for kk in range(2):
            acc[kk] += product(1, kk, 2)
        write_y(0)
        factor_ready(3)
        arrived(y_in.at[2], Y_IN + 2)
        for kk in range(2):
            put_p(1, kk, acc[kk] + product(2, kk, 3))
        to_owner(1, 5)

        @pl.when(own)
        def _():
            solve_forward(1)
            solve_back(1)
            to_line(1, 6)

        arrived(x_in.at[1], X_IN + 1)
        for line in range(4):
            put_q(0, line, back_product(1, 3, line))
        to_supernode(0, 2, 0, 9)
        to_lines(1, 7)

        @pl.when(own)
        def _():
            to_plane(y_own.at[1], 1, 8, Y_ALL + 1)

        for line in range(4):
            put_q(1, line, back_product(1, 2, line))
        for line in range(4):
            q_acc[line] = back_product(1, 1, line)
        write_y(1)
        to_supernode(1, 0, 1, 10)
        write_x(1)

        @pl.when(own)
        def _():
            solve_back(0, 0, 1)
            to_line(0, 11)

        arrived(x_in.at[0], X_IN)
        for line in range(4):
            put_q(2, line, q_acc[line] + back_product(0, 0, line))
        to_supernode(2, 1, 0, 13)

        to_lines(0, 12)
        write_x(0)
        for index in range(4):
            factor_sent(index)
        sent_unless(own, 1, 2)
        sent_unless(own, 5, 2)
        sent(9, 4)
        sent(7, 7)
        sent(12, 7)
        sent_unless(own, 10, 4)
        sent(13, 4)

        @pl.when(source)
        def _():
            for core in range(2):
                share(core, False)

        @pl.when(own)
        def _():
            sent(3, 7)
            sent_unless(source, 4, 16)
            sent(6, 3)
            sent_unless(source, 8, 16)
            sent(11, 3)


def per_device(factor, pattern, dinv, rhs):
    bf16, f32 = jnp.bfloat16, jnp.float32
    vmem = pl.BlockSpec(memory_space=pltpu.VMEM)
    result = pl.pallas_call(
        kernel,
        out_shape=jax.ShapeDtypeStruct((2, 2, 256, 256), bf16),
        in_specs=[pl.BlockSpec(memory_space=pltpu.HBM)] * 4,
        out_specs=vmem,
        scratch_shapes=[
            pltpu.SMEM((2, 4), jnp.int32),
            pltpu.VMEM((4, 256, 256), bf16),
            pltpu.VMEM((2, 256, 256), bf16),
            pltpu.VMEM((2, 256, 256), f32),
            pltpu.VMEM((2, 4, 4, 256, 256), bf16),
            pltpu.VMEM((2, 256, 256), bf16),
            pltpu.VMEM((2, 2, 32, 256), f32),
            pltpu.VMEM((2, 32, 256), f32),
            pltpu.VMEM((2, 32, 256), bf16),
            pltpu.VMEM((2, 32, 256), bf16),
            pltpu.VMEM((2, 32, 256), bf16),
            pltpu.VMEM((3, 4, 32, 256), bf16),
            pltpu.VMEM((2, 2, 32, 256), bf16),
            pltpu.VMEM((2, 4, 32, 256), bf16),
            pltpu.VMEM((2, 32, 256), f32),
            pltpu.VMEM((32, 32, 256), bf16),
            pltpu.VMEM((2, 2, 32, 256), bf16),
            pltpu.VMEM((256, 256), f32),
            pltpu.VMEM((4, 32, 256), f32),
            pltpu.VMEM((3, 4, 32, 256), bf16),
            pltpu.VMEM((3, 8, 32, 256), bf16),
            pltpu.SemaphoreType.DMA((24,)),
            pltpu.SemaphoreType.DMA((28,)),
            pltpu.SemaphoreType.DMA((7,)),
        ],
        compiler_params=pltpu.CompilerParams(
            collective_id=0, has_side_effects=True, vmem_limit_bytes=60 * 1024 * 1024
        ),
        cost_estimate=pl.CostEstimate(flops=600_000_000, bytes_accessed=3_000_000, transcendentals=0),
    )(pattern[:, 0, :, 0], factor[:, 0, :, 0], dinv[:, 0], rhs[:, 0])
    return result[0][:, None], result[1][:, None]


def solution(mesh):
    placed = (
        P(None, "row", None, "col", None, None),
        P(None, "row", None, "col"),
        P(None, "row", None, None),
        P(None, "row", None, None),
    )
    return jax.shard_map(
        per_device,
        mesh=mesh,
        in_specs=placed,
        out_specs=(P(None, "row", None, None), P(None, "row", None, None)),
        check_vma=False,
    )
```

```python
import jax
import jax.numpy as jnp
from jax import lax
from jax.experimental import pallas as pl
from jax.experimental.pallas import tpu as pltpu
from jax.sharding import PartitionSpec as P

MESH = pl.DeviceIdType.MESH
NT = (((1,), (1,)), ((), ()))
NN = (((1,), (0,)), ((), ()))
PLACES = ((0, 0), (1, 0), (1, 1), (1, 2))
Y_IN, P_IN, Y_ALL, X_IN, X_ALL, Q_IN, L_IN, G_IN, D_IN, B_IN, Y0_IN, G_0 = 0, 3, 5, 7, 9, 11, 14, 18, 22, 23, 24, 25


def exact_dot(lhs, inverse, dims):
    rows = lhs.shape[0]
    high = lhs.astype(jnp.bfloat16)
    rest = lhs - high.astype(jnp.float32)
    mid = rest.astype(jnp.bfloat16)
    low = (rest - mid.astype(jnp.float32)).astype(jnp.bfloat16)
    stacked = jnp.concatenate([high, mid, low], axis=0)
    out = lax.dot_general(stacked, inverse, dims, preferred_element_type=jnp.float32)
    return out[:rows] + (out[rows : 2 * rows] + out[2 * rows :])


def kernel(
    pattern_hbm, factor_hbm, dinv_hbm, rhs_hbm, out,
    pattern, factor, dinv, rhs, blocks, d_own, b_t, b_own, y_0, y_own, x_own, y_in, p_out, p_in, acc,
    full, x_in, turned, q_acc, q_out, q_in,
    send_sem, recv_sem, load_sem,
):
    r, c = lax.axis_index("row"), lax.axis_index("col")
    z, k = r // 2, r % 2
    h = z // 8
    s = r % 16
    x, y = c // 4, c % 4
    own = y // 2 == z % 2
    core_own = y % 2
    line_own = z % 8 // 2
    source = own & (k == core_own)
    barrier = pltpu.get_barrier_semaphore()
    loads = [
        pltpu.make_async_copy(source, target, load_sem.at[i])
        for i, (source, target) in enumerate(
            ((rhs_hbm, rhs), (dinv_hbm, dinv), (pattern_hbm, pattern))
            + tuple((factor_hbm.at[slot, level], factor.at[j]) for j, (slot, level) in enumerate(PLACES))
        )
    ]
    for load in loads:
        load.start()

    def signal(row, col):
        pl.semaphore_signal(barrier, inc=1, device_id=(row, col), device_id_type=MESH)

    @pl.loop(1, 32)
    def _(p):
        signal((r + p) % 32, c)

    @pl.loop(1, 16)
    def _(p):
        signal(r, (c + p) % 16)
        signal(2 * z + 1 - k, (c + p) % 16)

    def remote(src, dst, event, cls, row, col):
        return pltpu.make_async_remote_copy(
            src_ref=src, dst_ref=dst, send_sem=send_sem.at[event], recv_sem=recv_sem.at[cls],
            device_id=(row, col), device_id_type=MESH,
        )

    def send(src, dst, event, cls, row, col, here):
        @pl.when(here)
        def _():
            pltpu.make_async_copy(src, dst, recv_sem.at[cls]).start()

        @pl.when(jnp.logical_not(here))
        def _():
            remote(src, dst, event, cls, row, col).start()

    def arrived(buf, cls):
        remote(buf, buf, 0, cls, r, c).wait_recv()

    def sent(event, count):
        d = full.at[pl.ds(0, count)]
        remote(d, d, event, 0, r, c).wait_send()

    def sent_unless(here, event, count):
        @pl.when(here)
        def _():
            sent(event, count - 1)

        @pl.when(jnp.logical_not(here))
        def _():
            sent(event, count)

    def to_column(slot, level, half, event):
        def go(p, here):
            args = (y_own.at[slot], y_in.at[level, line_own], event, Y_IN + level,
                    2 * (8 * half + (z + p) % 8) + k, c)
            if here is None:
                remote(*args).start()
            else:
                send(*args, here)

        go(0, half == h)

        @pl.loop(1, 8)
        def _(p):
            go(p, None)

    def first_to_column(half, event):
        def go(p, core, here):
            args = (y_0.at[core], y_in.at[0, line_own], event, Y_IN,
                    2 * (8 * half + (z + p) % 8) + core, c)
            if here is None:
                remote(*args).start()
            else:
                send(*args, here)

        for core in range(2):
            go(0, core, (half == h) & (core == k))

        @pl.loop(1, 8)
        def _(p):
            for core in range(2):
                go(p, core, None)

    def to_owner(slot, event):
        for kk in range(2):
            send(p_out.at[slot, kk], p_in.at[slot, y], event, P_IN + slot, r, 4 * x + 2 * (z % 2) + kk,
                 own & (kk == core_own))

    def to_line(slot, event):
        pltpu.make_async_copy(x_own.at[slot], x_in.at[slot, core_own], recv_sem.at[X_IN + slot]).start()
        for p in range(1, 4):
            remote(x_own.at[slot], x_in.at[slot, core_own], event, X_IN + slot, r, 4 * x + (y + p) % 4).start()

    def to_plane(src, slot, event, cls):
        dst = full.at[8 * slot + 2 * x + k]
        row = 2 * z + core_own
        send(src, dst, event, cls, row, c, source)

        @pl.loop(1, 16)
        def _(p):
            remote(src, dst, event, cls, row, (c + p) % 16).start()

    def to_lines(slot, event):
        for p in range(4):
            for core in range(2):
                args = (x_in.at[slot, core], full.at[16 + 8 * slot + 2 * x + k], event, X_ALL + slot,
                        2 * z + core, 4 * ((x + p) % 4) + y)
                if p == 0:
                    send(*args, core == k)
                else:
                    remote(*args).start()

    def to_supernode(slot, cls, half, event):
        for p in range(4):
            line = (line_own + p) % 4
            args = (q_out.at[slot, line], q_in.at[cls, z % 8], event, Q_IN + cls,
                    2 * (8 * half + 2 * line + y // 2) + k, c)
            if p == 0:
                send(*args, own & (half == h))
            else:
                remote(*args).start()

    def share(core, start):
        pairs = [(dinv, d_own, D_IN), (b_t.at[core], b_own, B_IN)]
        for i, (src, dst, cls) in enumerate(pairs):
            if start:
                send(src, dst, 22 + i, cls, 2 * z + core, c, core == k)
            else:
                pl.when(core != k)(remote(src, dst, 22 + i, cls, 2 * z + core, c).wait_send)

    def gather(index):
        block = blocks.at[k, index, x]
        for p in (2, 1, 3):
            cls = G_0 + p - 1 if index == 0 else G_IN + index
            remote(block, block, 14 + index, cls, r, 4 * ((x + p) % 4) + y).start()
        swap(index, x).start()

    def swap(index, line):
        block = blocks.at[k, index, line]
        return remote(block, block, 18 + index, L_IN + index, 2 * z + 1 - k, c)

    def gathered(index):
        if index > 0:
            arrived(blocks.at[k, index, pl.ds(0, 3)], G_IN + index)
        for p in (1, 3, 2):
            line = (x + 4 - p) % 4
            if index == 0:
                arrived(blocks.at[k, index, line], G_0 + p - 1)
            swap(index, line).start()

    def factor_ready(index):
        arrived(blocks.at[1 - k, index], L_IN + index)

    def factor_sent(index):
        d = blocks.at[k, index, pl.ds(0, 3)]
        remote(d, d, 14 + index, 0, r, c).wait_send()
        d = blocks.at[k, index]
        remote(d, d, 18 + index, 0, r, c).wait_send()

    def product(level, kk, index):
        total = None
        for line in range(4):
            term = lax.dot_general(
                y_in[level, line], blocks[kk, index, line], NT,
                preferred_element_type=jnp.float32,
            )
            total = term if total is None else total + term
        return total

    def back_product(slot, index, line):
        total = None
        for kk in range(2):
            term = lax.dot_general(
                x_in[slot, kk], blocks[kk, index, line], NN,
                preferred_element_type=jnp.float32,
            )
            total = term if total is None else total + term
        return total

    def solve_forward(slot):
        arrived(p_in.at[slot], P_IN + slot)
        total = jnp.sum(p_in[slot].astype(jnp.float32), axis=0)
        y_own[slot] = exact_dot(b_own[slot] - total, d_own[slot], NT).astype(jnp.bfloat16)

    def back_total(cls):
        arrived(q_in.at[cls], Q_IN + cls)
        return jnp.sum(q_in[cls].astype(jnp.float32), axis=0)

    def solve_back(slot, *classes):
        residue = y_own[slot].astype(jnp.float32)
        for cls in classes:
            residue = residue - back_total(cls)
        x_own[slot] = exact_dot(residue, d_own[slot], NN).astype(jnp.bfloat16)

    def own_ready():
        arrived(d_own, D_IN)
        arrived(b_own, B_IN)

    def put_p(slot, kk, value):
        p_out[slot, kk] = value.astype(jnp.bfloat16)

    def put_q(slot, line, value):
        q_out[slot, line] = value.astype(jnp.bfloat16)

    def natural(slot):
        value = full[pl.ds(8 * slot, 8)].reshape(256, 256)
        return value.astype(jnp.float32).T.astype(jnp.bfloat16)

    def write_y(slot):
        arrived(full.at[pl.ds(8 * slot, 8)], Y_ALL + slot)
        out[0, slot] = natural(slot)

    def write_x(slot):
        arrived(full.at[pl.ds(16 + 8 * slot, 8)], X_ALL + slot)
        out[1, slot] = natural(2 + slot)

    loads[0].wait()
    for slot in range(2):
        turned[...] = rhs[slot].T
        for core in range(2):
            b_t[core, slot] = turned[pl.ds(pl.multiple_of(64 * x + 32 * core, 32), 32), :]

    loads[1].wait()

    @pl.when(h == 0)
    def _():
        for core in range(2):
            y_0[core] = exact_dot(b_t[core, 0], dinv[0], NT).astype(jnp.bfloat16)

    for load in loads[2:]:
        load.wait()
    for index, (slot, level) in enumerate(PLACES):
        weight = pattern[slot, level].astype(jnp.float32)
        blocks[k, index, x] = (factor[index].astype(jnp.float32) * weight).astype(jnp.bfloat16)

    pl.semaphore_wait(barrier, 61)

    @pl.when(h == 0)
    def _():
        @pl.when(source)
        def _():
            first_to_column(1, 1)
            for core in range(2):
                share(core, True)
                send(y_0.at[core], y_own.at[0], 0, Y0_IN, 2 * z + core, c, core == k)
            sent(1, 16)
            first_to_column(0, 2)

        gather(1)
        gather(2)
        out[0, 0] = exact_dot(rhs[0].T, dinv[0], NT).T.astype(jnp.bfloat16)
        gathered(1)
        gathered(2)
        factor_ready(1)
        arrived(y_in.at[0], Y_IN)
        for kk in range(2):
            acc[kk] = product(0, kk, 1)
        factor_ready(2)
        arrived(y_in.at[1], Y_IN + 1)
        for kk in range(2):
            put_p(1, kk, acc[kk] + product(1, kk, 2))
        to_owner(1, 3)

        @pl.when(own)
        def _():
            own_ready()
            arrived(y_own.at[0], Y0_IN)
            solve_forward(1)
            to_column(1, 2, 1, 4)
            sent(4, 8)
            to_plane(y_own.at[1], 1, 5, Y_ALL + 1)

        write_y(1)

        @pl.when(own)
        def _():
            solve_back(1, 2)
            to_line(1, 6)

        arrived(x_in.at[1], X_IN + 1)
        for line in range(4):
            put_q(0, line, back_product(1, 2, line))
        to_supernode(0, 1, 1, 8)
        for line in range(4):
            put_q(1, line, back_product(1, 1, line))

        to_lines(1, 7)
        to_supernode(1, 0, 0, 9)
        write_x(1)

        @pl.when(own)
        def _():
            solve_back(0, 0, 1)
            to_plane(x_own.at[0], 2, 10, X_ALL)

        write_x(0)
        for index in (1, 2):
            factor_sent(index)
        sent_unless(own, 3, 2)
        sent(8, 4)
        sent(7, 7)
        sent_unless(own, 9, 4)

        @pl.when(source)
        def _():
            sent(2, 15)
            sent(0, 1)
            for core in range(2):
                share(core, False)

        @pl.when(own)
        def _():
            sent_unless(source, 5, 16)
            sent(6, 3)
            sent_unless(source, 10, 16)

    @pl.when(h == 1)
    def _():
        gather(0)

        @pl.when(source)
        def _():
            for core in range(2):
                share(core, True)

        gathered(0)
        factor_ready(0)
        arrived(y_in.at[0], Y_IN)
        for kk in range(2):
            put_p(0, kk, product(0, kk, 0))
        to_owner(0, 1)
        for index in range(1, 4):
            gather(index)

        @pl.when(own)
        def _():
            own_ready()
            solve_forward(0)
            to_column(0, 1, 0, 2)
            sent(2, 8)
            to_column(0, 1, 1, 3)

        for index in range(1, 4):
            gathered(index)
        factor_ready(1)
        for kk in range(2):
            acc[kk] = product(0, kk, 1)

        @pl.when(own)
        def _():
            to_plane(y_own.at[0], 0, 4, Y_ALL)

        factor_ready(2)
        arrived(y_in.at[1], Y_IN + 1)
        for kk in range(2):
            acc[kk] += product(1, kk, 2)
        write_y(0)
        factor_ready(3)
        arrived(y_in.at[2], Y_IN + 2)
        for kk in range(2):
            put_p(1, kk, acc[kk] + product(2, kk, 3))
        to_owner(1, 5)

        @pl.when(own)
        def _():
            solve_forward(1)
            solve_back(1)
            to_line(1, 6)

        arrived(x_in.at[1], X_IN + 1)
        for line in range(4):
            put_q(0, line, back_product(1, 3, line))
        to_supernode(0, 2, 0, 9)
        to_lines(1, 7)

        @pl.when(own)
        def _():
            to_plane(y_own.at[1], 1, 8, Y_ALL + 1)

        for line in range(4):
            put_q(1, line, back_product(1, 2, line))
        for line in range(4):
            q_acc[line] = back_product(1, 1, line)
        write_y(1)
        to_supernode(1, 0, 1, 10)
        write_x(1)

        @pl.when(own)
        def _():
            solve_back(0, 0, 1)
            to_line(0, 11)

        arrived(x_in.at[0], X_IN)
        for line in range(4):
            put_q(2, line, q_acc[line] + back_product(0, 0, line))
        to_supernode(2, 1, 0, 13)

        to_lines(0, 12)
        write_x(0)
        for index in range(4):
            factor_sent(index)
        sent_unless(own, 1, 2)
        sent_unless(own, 5, 2)
        sent(9, 4)
        sent(7, 7)
        sent(12, 7)
        sent_unless(own, 10, 4)
        sent(13, 4)

        @pl.when(source)
        def _():
            for core in range(2):
                share(core, False)

        @pl.when(own)
        def _():
            sent(3, 7)
            sent_unless(source, 4, 16)
            sent(6, 3)
            sent_unless(source, 8, 16)
            sent(11, 3)


def per_device(factor, pattern, dinv, rhs):
    bf16, f32 = jnp.bfloat16, jnp.float32
    vmem = pl.BlockSpec(memory_space=pltpu.VMEM)
    result = pl.pallas_call(
        kernel,
        out_shape=jax.ShapeDtypeStruct((2, 2, 256, 256), bf16),
        in_specs=[pl.BlockSpec(memory_space=pltpu.HBM)] * 4,
        out_specs=vmem,
        scratch_shapes=[
            pltpu.SMEM((2, 4), jnp.int32),
            pltpu.VMEM((4, 256, 256), bf16),
            pltpu.VMEM((2, 256, 256), bf16),
            pltpu.VMEM((2, 256, 256), f32),
            pltpu.VMEM((2, 4, 4, 256, 256), bf16),
            pltpu.VMEM((2, 256, 256), bf16),
            pltpu.VMEM((2, 2, 32, 256), f32),
            pltpu.VMEM((2, 32, 256), f32),
            pltpu.VMEM((2, 32, 256), bf16),
            pltpu.VMEM((2, 32, 256), bf16),
            pltpu.VMEM((2, 32, 256), bf16),
            pltpu.VMEM((3, 4, 32, 256), bf16),
            pltpu.VMEM((2, 2, 32, 256), bf16),
            pltpu.VMEM((2, 4, 32, 256), bf16),
            pltpu.VMEM((2, 32, 256), f32),
            pltpu.VMEM((32, 32, 256), bf16),
            pltpu.VMEM((2, 2, 32, 256), bf16),
            pltpu.VMEM((256, 256), f32),
            pltpu.VMEM((4, 32, 256), f32),
            pltpu.VMEM((3, 4, 32, 256), bf16),
            pltpu.VMEM((3, 8, 32, 256), bf16),
            pltpu.SemaphoreType.DMA((24,)),
            pltpu.SemaphoreType.DMA((28,)),
            pltpu.SemaphoreType.DMA((7,)),
        ],
        compiler_params=pltpu.CompilerParams(
            collective_id=0, has_side_effects=True, vmem_limit_bytes=60 * 1024 * 1024
        ),
        cost_estimate=pl.CostEstimate(flops=600_000_000, bytes_accessed=3_000_000, transcendentals=0),
    )(pattern[:, 0, :, 0], factor[:, 0, :, 0], dinv[:, 0], rhs[:, 0])
    return result[0][:, None], result[1][:, None]


def solution(mesh):
    placed = (
        P(None, "row", None, "col", None, None),
        P(None, "row", None, "col"),
        P(None, "row", None, None),
        P(None, "row", None, None),
    )
    return jax.shard_map(
        per_device,
        mesh=mesh,
        in_specs=placed,
        out_specs=(P(None, "row", None, None), P(None, "row", None, None)),
        check_vma=False,
    )
```
